256 devices in a mesh: section: 4 (over y), dp: 2 (over x_hi), tensor: 32 (over x_lo, z, core).
Axes of the slice: x: 4 (x_hi: 2, x_lo: 2; x = x_hi * 2 + x_lo), y: 4, z: 8, core: 2. Of those that a mesh axis runs over, the one named last changes fastest.
Arguments:
- weights: bfloat16 [4, 6144, 24576], P('section', 'dp', 'tensor'), may hold values from -0.078125 to 0.078125
- arriving: bfloat16 [4, 2, 512, 6144], P('section', None, ('dp', 'tensor')), may hold values from -50 to 50
- vectors: float32 [4, 6144], P('section'), may hold values from 0.25 to 1.75
Outputs:
- leaving: bfloat16 [4, 2, 512, 6144], P('section', None, ('dp', 'tensor'))
- weight_grads: bfloat16 [4, 6144, 24576], P('section', 'dp', 'tensor')
- vector_grads: float32 [4, 6144], P('section')
The draws below stay inside these ranges and needn't reach their ends.
All inputs are finite; a program needn't handle non-finite values.
Results may differ from the reference program's by a relative error of at most 0.024.
Values may be sent and summed in bfloat16 or wider, within the bound.
A program may use at most 128 MiB of HBM per device.

```python
import math
import jax
import jax.numpy as jnp
from jax import lax

D = 6144
FF = 24576
MICRO = 2
TOK = 256
TOKENS = 512
N_SECTION = 4
N_DP = 2
N_TENSOR = 32


def draw_arriving(key, part):
    key = jax.random.fold_in(key, 7)
    key_rows, key_cols, key_base = jax.random.split(key, 3)
    shape = (N_SECTION, MICRO, TOKENS, D)
    row_scale = jnp.exp(jax.random.uniform(key_rows, (N_SECTION, MICRO, TOKENS, 1), jnp.float32, 0.0, math.log(10.0))) / math.sqrt(10.0)
    col_scale = jnp.exp(jax.random.uniform(key_cols, (N_SECTION, 1, 1, D), jnp.float32, 0.0, math.log(10.0))) / math.sqrt(10.0)
    values = jax.random.normal(key_base, shape, jnp.float32) * row_scale * col_scale
    return jnp.clip(values, -50.0, 50.0).astype(jnp.bfloat16)


def shard_levels(stream_key, dims, cuts, least, largest):
    level = 1.0
    for axis_at, shards_of in cuts:
        steps = jax.random.uniform(jax.random.fold_in(jax.random.fold_in(stream_key, 6), axis_at), (shards_of,), jnp.float32, least / len(cuts), largest / len(cuts))
        level = level * jnp.repeat(jnp.exp(steps), dims[axis_at] // shards_of).reshape((-1,) + (1,) * (len(dims) - 1 - axis_at))
    return level


def normal_values(stream_key, extent, deviation, reach, shards=(), kind=jnp.bfloat16):
    level = shard_levels(stream_key, extent, shards, -0.22, 0.18) if shards else 1.0
    drawn = jax.random.normal(stream_key, extent, jnp.float32) * deviation * level
    return jnp.minimum(jnp.maximum(drawn, -reach), reach).astype(kind)


def setup_inputs(seed: int = 0) -> dict:
    seeds = jax.random.split(jax.random.key(seed), 4)
    weights = normal_values(seeds[0], (N_SECTION, D, FF), D ** -0.5, 0.078125, ((0, 4), (1, 2), (2, 32)))
    arriving = draw_arriving(jax.random.fold_in(seeds[3], 71), 0)
    vectors = jnp.clip(1.0 + 0.15 * jax.random.normal(seeds[2], (N_SECTION, D), jnp.float32), 0.25, 1.75)
    return dict(weights=weights, arriving=arriving, vectors=vectors)


coeff = 0.7978845608028654

def gelu_value(inputs):
    inner = jnp.tanh(coeff * (inputs + 0.044715 * inputs * inputs * inputs))
    return 0.5 * inputs * (1.0 + inner)

def gelu_slope(inputs):
    inner = jnp.tanh(coeff * (inputs + 0.044715 * inputs * inputs * inputs))
    return 0.5 * (1.0 + inner) + 0.5 * inputs * (1.0 - inner * inner) * coeff * (1.0 + 3.0 * 0.044715 * inputs * inputs)

def block_sum(hidden, weight):
    block_width = FF // N_TENSOR

    def add_block(total, block):
        start = (block * block_width).astype(jnp.int32)
        left = lax.dynamic_slice_in_dim(hidden, start, block_width, 1)
        right = lax.dynamic_slice_in_dim(weight, start, block_width, 1)
        product = lax.dot_general(left, right, (((1,), (1,)), ((), ())), preferred_element_type=jnp.float32)
        rounded = lax.optimization_barrier(product.astype(jnp.bfloat16))
        return (total + rounded.astype(jnp.float32), None)
    start_total = jnp.zeros((hidden.shape[0], D), jnp.float32)
    total, _ = lax.scan(add_block, start_total, jnp.arange(N_TENSOR).astype(jnp.int32))
    return total

def replica_sum(left, right):
    left = left.reshape(MICRO, N_DP, TOK, left.shape[-1])
    right = right.reshape(MICRO, N_DP, TOK, right.shape[-1])
    total = jnp.zeros((left.shape[-1], right.shape[-1]), jnp.float32)
    for replica in range(N_DP):
        rows_left = left[:, replica].reshape(MICRO * TOK, left.shape[-1])
        rows_right = right[:, replica].reshape(MICRO * TOK, right.shape[-1])
        product = lax.dot_general(rows_left, rows_right, (((0,), (0,)), ((), ())), preferred_element_type=jnp.float32)
        rounded = lax.optimization_barrier(product.astype(jnp.bfloat16))
        total = total + rounded.astype(jnp.float32)
    return total

def reference(weights, arriving, vectors):
    leaving_list = []
    grad_list = []
    vector_list = []
    for layer_index in range(N_SECTION // 2):
        up_index = 2 * layer_index
        down_index = up_index + 1
        w_up = weights[up_index]
        w_down = weights[down_index]
        gain = vectors[up_index]
        bias = vectors[down_index]
        inputs = arriving[up_index].reshape(MICRO * TOKENS, D)
        cotangent = arriving[down_index].reshape(MICRO * TOKENS, D)
        values = inputs.astype(jnp.float32)
        centred = values - lax.optimization_barrier(jnp.mean(values, axis=-1, keepdims=True))
        scaled = lax.rsqrt(lax.optimization_barrier(jnp.mean(centred * centred, axis=-1, keepdims=True)) + 1e-05)
        standard = centred * scaled
        normed = (standard * gain).astype(jnp.bfloat16)
        preact = jnp.dot(normed, w_up, preferred_element_type=jnp.float32)
        hidden = gelu_value(preact).astype(jnp.bfloat16)
        grad_hidden = jnp.dot(cotangent, w_down, preferred_element_type=jnp.float32).astype(jnp.bfloat16)
        pre_grad = (grad_hidden.astype(jnp.float32) * gelu_slope(preact)).astype(jnp.bfloat16)
        forward_sum = block_sum(hidden, w_down)
        backward_sum = block_sum(pre_grad, w_up)
        output = (values + forward_sum + bias).astype(jnp.bfloat16)
        grad_norm = backward_sum * gain
        mean_grad = lax.optimization_barrier(jnp.mean(grad_norm, axis=-1, keepdims=True))
        mean_mix = lax.optimization_barrier(jnp.mean(grad_norm * standard, axis=-1, keepdims=True))
        through = (grad_norm - mean_grad - standard * mean_mix) * scaled
        input_grad = (cotangent.astype(jnp.float32) + through).astype(jnp.bfloat16)
        leaving_list.append(input_grad.reshape(MICRO, TOKENS, D))
        leaving_list.append(output.reshape(MICRO, TOKENS, D))
        grad_list.append(replica_sum(normed, pre_grad).astype(jnp.bfloat16))
        grad_list.append(replica_sum(cotangent, hidden).astype(jnp.bfloat16))
        vector_list.append(lax.optimization_barrier(jnp.sum(backward_sum * standard, axis=0)))
        vector_list.append(lax.optimization_barrier(jnp.sum(cotangent.astype(jnp.float32), axis=0)))
    return (jnp.stack(leaving_list), jnp.stack(grad_list), jnp.stack(vector_list))
```

```python
import jax
import jax.numpy as jnp
from jax import lax
from jax.sharding import PartitionSpec as P

coeff = 0.7978845608028654


def swap(block, axis):
    count = lax.axis_size(axis)
    return lax.ppermute(block, axis, [(i, i ^ 1) for i in range(count)])


def gelu_value(inputs):
    inner = jnp.tanh(coeff * (inputs + 0.044715 * inputs * inputs * inputs))
    return 0.5 * inputs * (1.0 + inner)


def gelu_slope(inputs):
    inner = jnp.tanh(coeff * (inputs + 0.044715 * inputs * inputs * inputs))
    return 0.5 * (1.0 + inner) + 0.5 * inputs * (1.0 - inner * inner) * coeff * (
        1.0 + 3.0 * 0.044715 * inputs * inputs
    )


def local(weights, arriving, vectors):
    leading = lax.axis_index("section") % 2 == 0
    replica = lax.axis_index("dp")
    weight = weights[0]
    half, width = weight.shape
    gain = vectors[0]
    stream = arriving[0]
    micro, rows, model = stream.shape
    values = stream.astype(jnp.float32)
    centred = values - jnp.mean(values, axis=-1, keepdims=True)
    scaled = lax.rsqrt(jnp.mean(centred * centred, axis=-1, keepdims=True) + 1e-05)
    standard = centred * scaled
    normed = (standard * gain).astype(jnp.bfloat16)
    outgoing = jnp.where(leading, normed, stream)
    back_rows = swap(stream, "section")

    def split(block, index):
        return lax.dynamic_slice_in_dim(block, index * half, half, block.ndim - 1)

    kept = split(outgoing, replica)
    came = swap(split(outgoing, 1 - replica), "dp")
    sums, gathers, carries = [], [], []
    for m in range(micro):
        pair = jnp.concatenate([kept[m], came[m]], axis=0)
        gathered = lax.all_gather(pair, "tensor", axis=0, tiled=True)
        gathered = gathered.reshape(-1, 2, rows, half)
        first = gathered[:, 0]
        second = gathered[:, 1]
        gathered = jnp.concatenate(
            [jnp.where(replica == 0, first, second), jnp.where(replica == 0, second, first)], axis=0
        ).reshape(-1, half)
        partial = jnp.dot(gathered, weight, preferred_element_type=jnp.float32)
        preact = partial + swap(partial.astype(jnp.bfloat16), "dp").astype(jnp.float32)
        outbound = jnp.where(leading, gelu_value(preact), preact).astype(jnp.bfloat16)
        back_hidden = swap(outbound, "section")
        carried = jnp.where(
            leading,
            (back_hidden.astype(jnp.float32) * gelu_slope(preact)).astype(jnp.bfloat16),
            back_hidden,
        )
        product = lax.dot_general(
            carried, weight, (((1,), (1,)), ((), ())), preferred_element_type=jnp.float32
        ).astype(jnp.bfloat16)
        product = jnp.transpose(product.reshape(2, -1, rows, half), (1, 0, 2, 3)).reshape(-1, half)
        total = lax.psum_scatter(product, "tensor", scatter_dimension=0, tiled=True)
        sums.append(total.reshape(2, rows, half))
        gathers.append(gathered)
        carries.append(carried)
    total = jnp.stack(sums, axis=1)
    mine = lax.dynamic_index_in_dim(total, replica, 0, False)
    theirs = swap(lax.dynamic_index_in_dim(total, 1 - replica, 0, False), "dp")
    summed = jnp.concatenate(
        [jnp.where(replica == 0, mine, theirs), jnp.where(replica == 0, theirs, mine)], axis=-1
    ).astype(jnp.float32)
    grad_norm = summed * gain
    mean_grad = jnp.mean(grad_norm, axis=-1, keepdims=True)
    mean_mix = jnp.mean(grad_norm * standard, axis=-1, keepdims=True)
    through = (grad_norm - mean_grad - standard * mean_mix) * scaled
    residual = back_rows.astype(jnp.float32)
    leaving = jnp.where(leading, residual + through, residual + summed + gain).astype(jnp.bfloat16)
    vector_term = jnp.where(
        leading, jnp.sum(summed * standard, axis=(0, 1)), jnp.sum(values, axis=(0, 1))
    )
    weight_grad = lax.dot_general(
        jnp.concatenate(gathers, axis=0),
        jnp.concatenate(carries, axis=0),
        (((0,), (0,)), ((), ())),
        preferred_element_type=jnp.float32,
    ).astype(jnp.bfloat16)
    totals = lax.psum(vector_term, ("dp", "tensor"))
    return (leaving[None], weight_grad[None], totals[None])


def solution(mesh):
    placed = (
        P("section", "dp", "tensor"),
        P("section", None, ("dp", "tensor"), None),
        P("section", None),
    )
    return jax.shard_map(
        local,
        mesh=mesh,
        in_specs=placed,
        out_specs=(
            P("section", None, ("dp", "tensor"), None),
            P("section", "dp", "tensor"),
            P("section", None),
        ),
        check_vma=False,
    )
```

```python
import functools

import jax
import jax.numpy as jnp
from jax import lax
from jax.experimental import pallas as pl
from jax.experimental.pallas import tpu as pltpu
from jax.sharding import PartitionSpec as P

coeff = 0.7978845608028654
BF = jnp.bfloat16
F32 = jnp.float32
NZ = 8
UP, DOWN = 0, 1


def steps_of(phase, way):
    return 4 if phase == way else 3


def kernel(
    weight_hbm, rows_ref, vec_ref,
    leave_ref, grad_hbm, total_ref,
    w_ref, stage, standard, scale, resid, a_ref,
    part, part_out, part_in, hid_out, hid_in, carried,
    y_own, y_out, y_in, ring_in, wg, tot, back, summed,
    v_out, v_group, v_mid, v_z, v_res, v_all,
    w_sem, wg_sem, group_s, group_r, resid_sem, ag_s, ag_r, sib_s, sib_r,
    dp_s, dp_r, sec_s, sec_r, y_s, y_r, rs_s, rs_r, fin_s, fin_r,
    vg_s, vg_r, vz_s, vz_r, vf_s, vf_r,
):
    sec = lax.axis_index("section")
    rep = lax.axis_index("dp")
    ten = lax.axis_index("tensor")
    core = lax.rem(ten, 2)
    z = lax.rem(lax.div(ten, 2), NZ)
    xlo = lax.div(ten, 2 * NZ)
    x = rep * 2 + xlo
    me = x * 2 + core
    leading = lax.rem(sec, 2) == 0
    model = rows_ref.shape[1]
    quarter = model // 4
    width = w_ref.shape[1]
    partner_sec = sec + 1 - 2 * lax.rem(sec, 2)

    def device(xx, zz, cc):
        return (sec, lax.div(xx, 2), (lax.rem(xx, 2) * NZ + zz) * 2 + cc)

    def member(j):
        return device(lax.div(j, 2), z, lax.rem(j, 2))

    above = device(x, lax.rem(z + 1, NZ), core)
    below = device(x, lax.rem(z + NZ - 1, NZ), core)
    sibling = device(x, z, 1 - core)
    dp_mate = (sec, 1 - rep, ten)
    sec_mate = (partner_sec, rep, ten)

    def copy(src, dst, send, recv, target):
        return pltpu.make_async_remote_copy(
            src_ref=src, dst_ref=dst, send_sem=send, recv_sem=recv,
            device_id=target, device_id_type=pl.DeviceIdType.MESH,
        )

    def zblock(o):
        return lax.rem(z + o, NZ)

    sent = []

    def start(c):
        c.start()
        sent.append(c)

    barrier = pltpu.get_barrier_semaphore()
    friends = [member(lax.rem(me + o, 8)) for o in range(1, 8)]
    friends += [device(x, zblock(o), core) for o in range(1, NZ)]
    friends += [sec_mate]
    for f in friends:
        pl.semaphore_signal(barrier, inc=1, device_id=f, device_id_type=pl.DeviceIdType.MESH)
    w_copy = pltpu.make_async_copy(weight_hbm, w_ref, w_sem)
    w_copy.start()

    @pl.when(leading)
    def _():
        acc = jnp.zeros((16, 1), F32)
        for q in range(4):
            acc += jnp.sum(rows_ref[:, q * quarter:(q + 1) * quarter].astype(F32), axis=1, keepdims=True)
        mean = acc / model
        acc = jnp.zeros((16, 1), F32)
        for q in range(4):
            cen = rows_ref[:, q * quarter:(q + 1) * quarter].astype(F32) - mean
            acc += jnp.sum(cen * cen, axis=1, keepdims=True)
        rs = lax.rsqrt(acc / model + 1e-05)
        scale[...] = jnp.broadcast_to(rs, scale.shape)
        for q in range(4):
            cols = slice(q * quarter, (q + 1) * quarter)
            std = (rows_ref[:, cols].astype(F32) - mean) * rs
            standard[:, cols] = std
            stage[q] = (std * vec_ref[:, cols]).astype(BF)

    @pl.when(jnp.logical_not(leading))
    def _():
        for q in range(4):
            stage[q] = rows_ref[:, q * quarter:(q + 1) * quarter]

    pl.semaphore_wait(barrier, len(friends))

    my_rows = pl.ds(pl.multiple_of(x * 16, 16), 16)
    for o in range(1, 8):
        j = lax.rem(me + o, 8)
        q = lax.div(j, 4) * 2 + lax.rem(j, 2)
        start(copy(
            stage.at[q], a_ref.at[lax.rem(j, 2), core, z, my_rows],
            group_s.at[o], group_r.at[me], member(j),
        ))
    a_ref[core, core, z, my_rows] = stage[rep * 2 + core]
    start(copy(rows_ref, resid, resid_sem.at[0], resid_sem.at[1], sec_mate))

    def group_wait(phase):
        for o in range(4):
            xx = lax.rem(x + o, 4)
            piece = a_ref.at[core, phase, z, pl.ds(pl.multiple_of(xx * 16, 16), 16)]
            sender = xx * 2 + phase

            def wait():
                copy(piece, piece, group_s.at[0], group_r.at[sender], member(sender)).wait_recv()

            if o:
                wait()
            else:
                pl.when(core != phase)(wait)

    def ag_send(phase, way, k):
        o = (NZ - k) % NZ if way == UP else k
        block = a_ref.at[core, phase, zblock(o)]
        start(copy(
            block, block, ag_s.at[phase, way, k], ag_r.at[phase, way, k],
            above if way == UP else below,
        ))

    def ag_wait(phase, way, k):
        o = NZ - 1 - k if way == UP else k + 1
        block = a_ref.at[core, phase, zblock(o)]
        copy(
            block, block, ag_s.at[phase, way, k], ag_r.at[phase, way, k],
            above if way == UP else below,
        ).wait_recv()
        return o

    def sib_send(phase, o):
        block = a_ref.at[core, phase, zblock(o)]
        start(copy(block, block, sib_s.at[phase, o], sib_r.at[phase, o], sibling))

    def sib_wait(phase, o):
        block = a_ref.at[1 - core, phase, zblock(o)]
        copy(block, block, sib_s.at[phase, o], sib_r.at[phase, o], sibling).wait_recv()

    def forward(phase, j):
        for way in (UP, DOWN):
            count = steps_of(phase, way)
            if j > count:
                continue
            o = ag_wait(phase, way, j - 1)
            if j < count:
                ag_send(phase, way, j)
            sib_send(phase, o)

    def pair(k):
        return (NZ - k, k) if k < 4 else (4, 0)

    def mm1(phase, k):
        u = phase * 4 + k - 1
        o1, o2 = pair(k)
        sib_wait(phase, o1)
        sib_wait(phase, o2)
        b1, b2 = zblock(o1), zblock(o2)

        @pl.loop(0, width // 256)
        def _(n):
            cols = pl.ds(pl.multiple_of(n * 256, 256), 256)
            acc = None
            for q in range(2):
                left = jnp.concatenate([a_ref[q, phase, b1], a_ref[q, phase, b2]], axis=0)
                d = jnp.dot(left, w_ref[q * quarter:(q + 1) * quarter, cols], preferred_element_type=F32)
                acc = d if acc is None else acc + d
            part[u, :, cols] = acc
            part_out[u, :, cols] = acc.astype(BF)

        start(copy(part_out.at[u], part_in.at[u], dp_s.at[u], dp_r.at[u], dp_mate))

    def mid1(phase, k):
        u = phase * 4 + k - 1
        copy(part_out.at[u], part_in.at[u], dp_s.at[u], dp_r.at[u], dp_mate).wait_recv()

        @pl.when(leading)
        def _():
            @pl.loop(0, 8)
            def _(n):
                rows = pl.ds(pl.multiple_of(n * 16, 16), 16)
                p = part[u, rows, :] + part_in[u, rows, :].astype(F32)
                sq = p * p
                inner = jnp.tanh(coeff * (p + 0.044715 * sq * p))
                one = 1.0 + inner
                hid_out[u, rows, :] = (0.5 * p * one).astype(BF)
                part[u, rows, :] = 0.5 * one + 0.5 * p * (1.0 - inner * inner) * coeff * (
                    1.0 + 3.0 * 0.044715 * sq
                )

        @pl.when(jnp.logical_not(leading))
        def _():
            @pl.loop(0, 8)
            def _(n):
                rows = pl.ds(pl.multiple_of(n * 16, 16), 16)
                hid_out[u, rows, :] = (part[u, rows, :] + part_in[u, rows, :].astype(F32)).astype(BF)

        start(copy(hid_out.at[u], hid_in.at[u], sec_s.at[u], sec_r.at[u], sec_mate))

    def mid2(phase, k):
        u = phase * 4 + k - 1
        copy(hid_out.at[u], hid_in.at[u], sec_s.at[u], sec_r.at[u], sec_mate).wait_recv()
        for i, o in enumerate(pair(k)):
            b = zblock(o)

            @pl.when(leading)
            def _():
                @pl.loop(0, 4)
                def _(n):
                    src = pl.ds(pl.multiple_of(i * 64 + n * 16, 16), 16)
                    dst = pl.ds(pl.multiple_of(n * 16, 16), 16)
                    carried[phase, b, dst, :] = (hid_in[u, src, :].astype(F32) * part[u, src, :]).astype(BF)

            @pl.when(jnp.logical_not(leading))
            def _():
                carried[phase, b] = hid_in[u, i * 64:(i + 1) * 64, :]

    def mm2(phase, k):
        o1, o2 = pair(k)
        b1, b2 = zblock(o1), zblock(o2)
        for half, dst in ((1 - core, y_out), (core, y_own)):
            @pl.loop(0, quarter // 256)
            def _(n):
                left = jnp.concatenate([carried[phase, b1], carried[phase, b2]], axis=0)
                right = w_ref[pl.ds(pl.multiple_of(half * quarter + n * 256, 256), 256), :]
                d = lax.dot_general(
                    left, right, (((1,), (1,)), ((), ())), preferred_element_type=F32
                ).astype(BF)
                cols = pl.ds(pl.multiple_of(n * 256, 256), 256)
                dst[phase, o1, :, cols] = d[:64]
                dst[phase, o2, :, cols] = d[64:]

            if dst is y_out:
                for o in (o1, o2):
                    start(copy(
                        y_out.at[phase, o], y_in.at[phase, o], y_s.at[phase, o], y_r.at[phase, o], sibling
                    ))

    def y_wait(phase, o):
        copy(
            y_out.at[phase, o], y_in.at[phase, o], y_s.at[phase, o], y_r.at[phase, o], sibling
        ).wait_recv()

    def rs_copy(phase, way, i):
        count = steps_of(phase, way)
        o = count - i if way == UP else NZ - (count - i)
        return o, copy(
            y_own.at[phase, o], ring_in.at[phase, way, i], rs_s.at[phase, way, i], rs_r.at[phase, way, i],
            above if way == UP else below,
        )

    def rs_step(phase, way, i):
        o, c = rs_copy(phase, way, i)
        y_wait(phase, o)
        if i:
            rs_copy(phase, way, i - 1)[1].wait_recv()

        @pl.loop(0, 4)
        def _(n):
            rows = pl.ds(pl.multiple_of(n * 16, 16), 16)
            s = y_own[phase, o, rows, :].astype(F32) + y_in[phase, o, rows, :].astype(F32)
            if i:
                s += ring_in[phase, way, i - 1, rows, :].astype(F32)
            y_own[phase, o, rows, :] = s.astype(BF)

        start(c)

    def rs_final(phase):
        y_wait(phase, 0)
        last = [steps_of(phase, way) - 1 for way in (UP, DOWN)]
        for way in (UP, DOWN):
            rs_copy(phase, way, last[way])[1].wait_recv()

        @pl.loop(0, 4)
        def _(n):
            rows = pl.ds(pl.multiple_of(n * 16, 16), 16)
            s = y_own[phase, 0, rows, :].astype(F32) + y_in[phase, 0, rows, :].astype(F32)
            for way in (UP, DOWN):
                s += ring_in[phase, way, last[way], rows, :].astype(F32)
            tot[phase, rows, :] = s.astype(BF)

        for o in range(4):
            xx = lax.rem(x + o, 4)
            piece = tot.at[phase, pl.ds(pl.multiple_of(xx * 16, 16), 16)]
            c = copy(
                piece, back.at[me], fin_s.at[phase, o], fin_r.at[me], device(xx, z, phase)
            )
            if o:
                start(c)
            else:
                @pl.when(core != phase)
                def _():
                    c.start()

                @pl.when(core == phase)
                def _():
                    back[me] = tot[phase, my_rows, :]

    def wgrad(first, count):
        @pl.loop(first, first + count)
        def _(t):
            q = lax.div(t, quarter // 256)
            cols = pl.ds(pl.multiple_of(lax.rem(t, quarter // 256) * 256, 256), 256)
            left = a_ref[q, :, :, :, cols].reshape(-1, 256)
            right = carried[...].reshape(-1, width)
            d = lax.dot_general(left, right, (((0,), (0,)), ((), ())), preferred_element_type=F32)
            wg[pl.ds(pl.multiple_of(t * 256, 256), 256), :] = d.astype(BF)

    for phase in (0, 1):
        group_wait(phase)
        ag_send(phase, UP, 0)
        ag_send(phase, DOWN, 0)
        sib_send(phase, 0)
    w_copy.wait()
    for j in range(1, 5):
        for phase in (0, 1):
            forward(phase, j)
            mm1(phase, j)
        if j >= 3:
            for phase in (0, 1):
                mid2(phase, j - 2)
                mm2(phase, j - 2)
        if j >= 2:
            for phase in (0, 1):
                mid1(phase, j - 1)
    for phase in (0, 1):
        mid1(phase, 4)
    for phase in (0, 1):
        mid2(phase, 3)
        mm2(phase, 3)
    for phase in (0, 1):
        mid2(phase, 4)
        mm2(phase, 4)
        rs_step(phase, UP, 0)
        rs_step(phase, DOWN, 0)
    tiles = model // 512
    per = tiles // 4
    copies = []
    for i in range(1, 5):
        wgrad((i - 1) * per, per)
        rows = pl.ds((i - 1) * per * 256, per * 256)
        c = pltpu.make_async_copy(wg.at[rows], grad_hbm.at[rows], wg_sem.at[i - 1])
        c.start()
        copies.append(c)
        for phase in (0, 1):
            for way in (UP, DOWN):
                if i < steps_of(phase, way):
                    rs_step(phase, way, i)
    for phase in (0, 1):
        rs_final(phase)

    copy(rows_ref, resid, resid_sem.at[0], resid_sem.at[1], sec_mate).wait_recv()
    for o in range(1, 8):
        j = lax.rem(me + o, 8)
        copy(back.at[j], back.at[j], fin_s.at[0, 0], fin_r.at[j], member(j)).wait_recv()

    def quarter_sum(q):
        j = (q // 2) * 4 + q % 2
        return back[j].astype(F32) + back[j + 2].astype(F32)

    chunk = model // 8

    @pl.when(leading)
    def _():
        mean = jnp.zeros((16, 1), F32)
        mix = jnp.zeros((16, 1), F32)
        for q in range(4):
            cols = slice(q * quarter, (q + 1) * quarter)
            s = quarter_sum(q)
            std = standard[:, cols]
            v = jnp.sum(s * std, axis=0, keepdims=True)
            v_out[2 * q] = v[:, :chunk]
            v_out[2 * q + 1] = v[:, chunk:]
            g = s * vec_ref[:, cols]
            summed[:, cols] = g
            mean += jnp.sum(g, axis=1, keepdims=True)
            mix += jnp.sum(g * std, axis=1, keepdims=True)
        mean = mean / model
        mix = mix / model
        rs = scale[:, 0:1]
        for q in range(4):
            cols = slice(q * quarter, (q + 1) * quarter)
            through = (summed[:, cols] - mean - standard[:, cols] * mix) * rs
            leave_ref[:, cols] = (resid[:, cols].astype(F32) + through).astype(BF)

    @pl.when(jnp.logical_not(leading))
    def _():
        for q in range(4):
            cols = slice(q * quarter, (q + 1) * quarter)
            v = jnp.sum(rows_ref[:, cols].astype(F32), axis=0, keepdims=True)
            v_out[2 * q] = v[:, :chunk]
            v_out[2 * q + 1] = v[:, chunk:]
            leave_ref[:, cols] = (resid[:, cols].astype(F32) + quarter_sum(q) + vec_ref[:, cols]).astype(BF)

    for o in range(1, 8):
        j = lax.rem(me + o, 8)
        start(copy(v_out.at[j], v_group.at[me], vg_s.at[o], vg_r.at[me], member(j)))
    v_group[me] = v_out[me]
    for o in range(1, 8):
        j = lax.rem(me + o, 8)
        copy(v_group.at[j], v_group.at[j], vg_s.at[0], vg_r.at[j], member(j)).wait_recv()
    v_mid[...] = jnp.sum(v_group[...], axis=0)
    for o in range(1, NZ):
        start(copy(v_mid, v_z.at[z], vz_s.at[o], vz_r.at[z], device(x, zblock(o), core)))
    v_z[z] = v_mid[...]
    for o in range(1, NZ):
        b = zblock(o)
        copy(v_z.at[b], v_z.at[b], vz_s.at[0], vz_r.at[b], device(x, b, core)).wait_recv()
    v_res[...] = jnp.sum(v_z[...], axis=0)
    for o in range(1, 8):
        j = lax.rem(me + o, 8)
        start(copy(v_res, v_all.at[me], vf_s.at[o], vf_r.at[me], member(j)))
    v_all[me] = v_res[...]
    for o in range(1, 8):
        j = lax.rem(me + o, 8)
        copy(v_all.at[j], v_all.at[j], vf_s.at[0], vf_r.at[j], member(j)).wait_recv()
    for j in range(8):
        total_ref[:, j * chunk:(j + 1) * chunk] = v_all[j]

    for c in sent:
        c.wait_send()
    for phase in (0, 1):
        @pl.when(core != phase)
        def _():
            copy(
                tot.at[phase, my_rows], back.at[me], fin_s.at[phase, 0], fin_r.at[me], device(x, z, phase)
            ).wait_send()
    for c in copies:
        c.wait()


def local(weights, arriving, vectors):
    _, half, width = weights.shape
    _, micro, rows, model = arriving.shape
    quarter = model // 4
    chunk = model // 8
    dma = pltpu.SemaphoreType.DMA
    vm = pltpu.VMEM
    block = (64, quarter)
    leaving, weight_grad, totals = pl.pallas_call(
        kernel,
        out_shape=(
            jax.ShapeDtypeStruct((micro * rows, model), BF),
            jax.ShapeDtypeStruct((half, width), BF),
            jax.ShapeDtypeStruct((1, model), F32),
        ),
        in_specs=[
            pl.BlockSpec(memory_space=pl.ANY),
            pl.BlockSpec(memory_space=pltpu.VMEM),
            pl.BlockSpec(memory_space=pltpu.VMEM),
        ],
        out_specs=(
            pl.BlockSpec(memory_space=pltpu.VMEM),
            pl.BlockSpec(memory_space=pl.ANY),
            pl.BlockSpec(memory_space=pltpu.VMEM),
        ),
        scratch_shapes=[
            vm((half, width), BF),
            vm((4, 16, quarter), BF),
            vm((16, model), F32),
            vm((16, 128), F32),
            vm((16, model), BF),
            vm((2, 2, NZ, *block), BF),
            vm((8, 128, width), F32),
            vm((8, 128, width), BF),
            vm((8, 128, width), BF),
            vm((8, 128, width), BF),
            vm((8, 128, width), BF),
            vm((2, NZ, 64, width), BF),
            vm((2, NZ, *block), BF),
            vm((2, NZ, *block), BF),
            vm((2, NZ, *block), BF),
            vm((2, 2, 4, *block), BF),
            vm((half, width), BF),
            vm((2, *block), BF),
            vm((8, 16, quarter), BF),
            vm((16, model), F32),
            vm((8, 1, chunk), F32),
            vm((8, 1, chunk), F32),
            vm((1, chunk), F32),
            vm((NZ, 1, chunk), F32),
            vm((1, chunk), F32),
            vm((8, 1, chunk), F32),
            dma, dma((4,)), dma((8,)), dma((8,)), dma((2,)),
            dma((2, 2, 4)), dma((2, 2, 4)), dma((2, NZ)), dma((2, NZ)),
            dma((8,)), dma((8,)), dma((8,)), dma((8,)),
            dma((2, NZ)), dma((2, NZ)), dma((2, 2, 4)), dma((2, 2, 4)),
            dma((2, 4)), dma((8,)),
            dma((8,)), dma((8,)), dma((8,)), dma((8,)), dma((8,)), dma((8,)),
        ],
        compiler_params=pltpu.CompilerParams(
            collective_id=0, has_side_effects=True, vmem_limit_bytes=56 * 1024 * 1024
        ),
        cost_estimate=pl.CostEstimate(
            flops=3 * 2 * 1024 * half * width, bytes_accessed=4 * half * width, transcendentals=1024 * width
        ),
    )(weights[0], arriving[0].reshape(micro * rows, model), vectors)
    return (leaving.reshape(1, micro, rows, model), weight_grad[None], totals)


def solution(mesh):
    placed = (
        P("section", "dp", "tensor"),
        P("section", None, ("dp", "tensor"), None),
        P("section", None),
    )
    return jax.shard_map(
        local,
        mesh=mesh,
        in_specs=placed,
        out_specs=(
            P("section", None, ("dp", "tensor"), None),
            P("section", "dp", "tensor"),
            P("section", None),
        ),
        check_vma=False,
    )
```

```python
import functools

import jax
import jax.numpy as jnp
from jax import lax
from jax.experimental import pallas as pl
from jax.experimental.pallas import tpu as pltpu
from jax.sharding import PartitionSpec as P

coeff = 0.7978845608028654
BF = jnp.bfloat16
F32 = jnp.float32
NZ = 8
UP, DOWN = 0, 1


def steps_of(phase, way):
    return 4 if phase == way else 3


def kernel(
    weight_hbm, rows_ref, vec_ref,
    leave_ref, grad_hbm, total_ref,
    w_ref, stage, standard, scale, resid, a_ref,
    part, part_out, part_in, hid_out, hid_in, carried,
    y_own, y_out, y_in, ring_in, wg, tot, back, summed,
    v_out, v_in,
    w_sem, wg_sem, group_s, group_r, resid_sem, ag_s, ag_r, sib_s, sib_r,
    dp_s, dp_r, sec_s, sec_r, y_s, y_r, rs_s, rs_r, fin_s, fin_r,
    v_s, v_r,
):
    sec = lax.axis_index("section")
    rep = lax.axis_index("dp")
    ten = lax.axis_index("tensor")
    core = lax.rem(ten, 2)
    z = lax.rem(lax.div(ten, 2), NZ)
    xlo = lax.div(ten, 2 * NZ)
    x = rep * 2 + xlo
    me = x * 2 + core
    leading = lax.rem(sec, 2) == 0
    model = rows_ref.shape[1]
    quarter = model // 4
    width = w_ref.shape[1]
    partner_sec = sec + 1 - 2 * lax.rem(sec, 2)

    def device(xx, zz, cc):
        return (sec, lax.div(xx, 2), (lax.rem(xx, 2) * NZ + zz) * 2 + cc)

    def member(j):
        return device(lax.div(j, 2), z, lax.rem(j, 2))

    above = device(x, lax.rem(z + 1, NZ), core)
    below = device(x, lax.rem(z + NZ - 1, NZ), core)
    sibling = device(x, z, 1 - core)
    dp_mate = (sec, 1 - rep, ten)
    sec_mate = (partner_sec, rep, ten)

    def copy(src, dst, send, recv, target):
        return pltpu.make_async_remote_copy(
            src_ref=src, dst_ref=dst, send_sem=send, recv_sem=recv,
            device_id=target, device_id_type=pl.DeviceIdType.MESH,
        )

    def zblock(o):
        return lax.rem(z + o, NZ)

    sent = []

    def start(c):
        c.start()
        sent.append(c)

    barrier = pltpu.get_barrier_semaphore()
    friends = [member(lax.rem(me + o, 8)) for o in range(1, 8)]
    z2 = z + 2 - 4 * lax.rem(lax.div(z, 2), 2)
    doubling = [
        sibling, device(rep * 2 + 1 - xlo, z, core), device(x, z + 1 - 2 * lax.rem(z, 2), core),
        device(x, z2, core), device(x, zblock(4), core), dp_mate,
    ]
    friends += [above, below, doubling[3], doubling[4], sec_mate]
    for f in friends:
        pl.semaphore_signal(barrier, inc=1, device_id=f, device_id_type=pl.DeviceIdType.MESH)
    w_copy = pltpu.make_async_copy(weight_hbm, w_ref, w_sem)
    w_copy.start()

    @pl.when(leading)
    def _():
        acc = jnp.zeros((16, 1), F32)
        for q in range(4):
            acc += jnp.sum(rows_ref[:, q * quarter:(q + 1) * quarter].astype(F32), axis=1, keepdims=True)
        mean = acc / model
        acc = jnp.zeros((16, 1), F32)
        for q in range(4):
            cen = rows_ref[:, q * quarter:(q + 1) * quarter].astype(F32) - mean
            acc += jnp.sum(cen * cen, axis=1, keepdims=True)
        rs = lax.rsqrt(acc / model + 1e-05)
        scale[...] = jnp.broadcast_to(rs, scale.shape)
        for q in range(4):
            cols = slice(q * quarter, (q + 1) * quarter)
            std = (rows_ref[:, cols].astype(F32) - mean) * rs
            standard[:, cols] = std
            stage[q] = (std * vec_ref[:, cols]).astype(BF)

    @pl.when(jnp.logical_not(leading))
    def _():
        for q in range(4):
            stage[q] = rows_ref[:, q * quarter:(q + 1) * quarter]

    pl.semaphore_wait(barrier, len(friends))

    my_rows = pl.ds(pl.multiple_of(x * 16, 16), 16)
    for o in range(1, 8):
        j = lax.rem(me + o, 8)
        q = lax.div(j, 4) * 2 + lax.rem(j, 2)
        start(copy(
            stage.at[q], a_ref.at[lax.rem(j, 2), core, z, my_rows],
            group_s.at[o], group_r.at[me], member(j),
        ))
    a_ref[core, core, z, my_rows] = stage[rep * 2 + core]
    start(copy(rows_ref, resid, resid_sem.at[0], resid_sem.at[1], sec_mate))

    def group_wait(phase):
        for o in range(4):
            xx = lax.rem(x + o, 4)
            piece = a_ref.at[core, phase, z, pl.ds(pl.multiple_of(xx * 16, 16), 16)]
            sender = xx * 2 + phase

            def wait():
                copy(piece, piece, group_s.at[0], group_r.at[sender], member(sender)).wait_recv()

            if o:
                wait()
            else:
                pl.when(core != phase)(wait)

    def ag_send(phase, way, k):
        o = (NZ - k) % NZ if way == UP else k
        block = a_ref.at[core, phase, zblock(o)]
        start(copy(
            block, block, ag_s.at[phase, way, k], ag_r.at[phase, way, k],
            above if way == UP else below,
        ))

    def ag_wait(phase, way, k):
        o = NZ - 1 - k if way == UP else k + 1
        block = a_ref.at[core, phase, zblock(o)]
        copy(
            block, block, ag_s.at[phase, way, k], ag_r.at[phase, way, k],
            above if way == UP else below,
        ).wait_recv()
        return o

    def sib_send(phase, o):
        block = a_ref.at[core, phase, zblock(o)]
        start(copy(block, block, sib_s.at[phase, o], sib_r.at[phase, o], sibling))

    def sib_wait(phase, o):
        block = a_ref.at[1 - core, phase, zblock(o)]
        copy(block, block, sib_s.at[phase, o], sib_r.at[phase, o], sibling).wait_recv()

    def forward(phase, j):
        for way in (UP, DOWN):
            count = steps_of(phase, way)
            if j > count:
                continue
            o = ag_wait(phase, way, j - 1)
            if j < count:
                ag_send(phase, way, j)
            sib_send(phase, o)

    units = [((0, 0), (1, 0))]
    for k in (1, 2, 3):
        units += [((phase, NZ - k), (phase, k)) for phase in (0, 1)]
    units += [((0, 4), (1, 4))]

    def mm1(u):
        for phase, o in units[u]:
            sib_wait(phase, o)
        (p1, b1), (p2, b2) = [(phase, zblock(o)) for phase, o in units[u]]

        @pl.loop(0, width // 256)
        def _(n):
            cols = pl.ds(pl.multiple_of(n * 256, 256), 256)
            acc = None
            for q in range(2):
                left = jnp.concatenate([a_ref[q, p1, b1], a_ref[q, p2, b2]], axis=0)
                d = jnp.dot(left, w_ref[q * quarter:(q + 1) * quarter, cols], preferred_element_type=F32)
                acc = d if acc is None else acc + d
            part[u, :, cols] = acc
            part_out[u, :, cols] = acc.astype(BF)

        start(copy(part_out.at[u], part_in.at[u], dp_s.at[u], dp_r.at[u], dp_mate))

    def mid1(u):
        copy(part_out.at[u], part_in.at[u], dp_s.at[u], dp_r.at[u], dp_mate).wait_recv()

        @pl.when(leading)
        def _():
            @pl.loop(0, 8)
            def _(n):
                rows = pl.ds(pl.multiple_of(n * 16, 16), 16)
                p = part[u, rows, :] + part_in[u, rows, :].astype(F32)
                sq = p * p
                inner = jnp.tanh(coeff * (p + 0.044715 * sq * p))
                one = 1.0 + inner
                hid_out[u, rows, :] = (0.5 * p * one).astype(BF)
                part[u, rows, :] = 0.5 * one + 0.5 * p * (1.0 - inner * inner) * coeff * (
                    1.0 + 3.0 * 0.044715 * sq
                )

        @pl.when(jnp.logical_not(leading))
        def _():
            @pl.loop(0, 8)
            def _(n):
                rows = pl.ds(pl.multiple_of(n * 16, 16), 16)
                hid_out[u, rows, :] = (part[u, rows, :] + part_in[u, rows, :].astype(F32)).astype(BF)

        start(copy(hid_out.at[u], hid_in.at[u], sec_s.at[u], sec_r.at[u], sec_mate))

    def mid2(u):
        copy(hid_out.at[u], hid_in.at[u], sec_s.at[u], sec_r.at[u], sec_mate).wait_recv()
        for i, (phase, o) in enumerate(units[u]):
            b = zblock(o)

            @pl.when(leading)
            def _():
                @pl.loop(0, 4)
                def _(n):
                    src = pl.ds(pl.multiple_of(i * 64 + n * 16, 16), 16)
                    dst = pl.ds(pl.multiple_of(n * 16, 16), 16)
                    carried[phase, b, dst, :] = (hid_in[u, src, :].astype(F32) * part[u, src, :]).astype(BF)

            @pl.when(jnp.logical_not(leading))
            def _():
                carried[phase, b] = hid_in[u, i * 64:(i + 1) * 64, :]

    def mm2(u):
        (p1, o1), (p2, o2) = units[u]
        b1, b2 = zblock(o1), zblock(o2)
        for half, dst in ((1 - core, y_out), (core, y_own)):
            @pl.loop(0, quarter // 256)
            def _(n):
                left = jnp.concatenate([carried[p1, b1], carried[p2, b2]], axis=0)
                right = w_ref[pl.ds(pl.multiple_of(half * quarter + n * 256, 256), 256), :]
                d = lax.dot_general(
                    left, right, (((1,), (1,)), ((), ())), preferred_element_type=F32
                ).astype(BF)
                cols = pl.ds(pl.multiple_of(n * 256, 256), 256)
                dst[p1, o1, :, cols] = d[:64]
                dst[p2, o2, :, cols] = d[64:]

            if dst is y_out:
                for phase, o in units[u]:
                    start(copy(
                        y_out.at[phase, o], y_in.at[phase, o], y_s.at[phase, o], y_r.at[phase, o], sibling
                    ))

    def y_wait(phase, o):
        copy(
            y_out.at[phase, o], y_in.at[phase, o], y_s.at[phase, o], y_r.at[phase, o], sibling
        ).wait_recv()

    def rs_copy(phase, way, i):
        count = steps_of(phase, way)
        o = count - i if way == UP else NZ - (count - i)
        return o, copy(
            y_own.at[phase, o], ring_in.at[phase, way, i], rs_s.at[phase, way, i], rs_r.at[phase, way, i],
            above if way == UP else below,
        )

    def rs_step(phase, way, i):
        o, c = rs_copy(phase, way, i)
        y_wait(phase, o)
        if i:
            rs_copy(phase, way, i - 1)[1].wait_recv()

        @pl.loop(0, 4)
        def _(n):
            rows = pl.ds(pl.multiple_of(n * 16, 16), 16)
            s = y_own[phase, o, rows, :].astype(F32) + y_in[phase, o, rows, :].astype(F32)
            if i:
                s += ring_in[phase, way, i - 1, rows, :].astype(F32)
            y_own[phase, o, rows, :] = s.astype(BF)

        start(c)

    def rs_final(phase):
        y_wait(phase, 0)
        last = [steps_of(phase, way) - 1 for way in (UP, DOWN)]
        for way in (UP, DOWN):
            rs_copy(phase, way, last[way])[1].wait_recv()

        @pl.loop(0, 4)
        def _(n):
            rows = pl.ds(pl.multiple_of(n * 16, 16), 16)
            s = y_own[phase, 0, rows, :].astype(F32) + y_in[phase, 0, rows, :].astype(F32)
            for way in (UP, DOWN):
                s += ring_in[phase, way, last[way], rows, :].astype(F32)
            tot[phase, rows, :] = s.astype(BF)

        for o in range(4):
            xx = lax.rem(x + o, 4)
            piece = tot.at[phase, pl.ds(pl.multiple_of(xx * 16, 16), 16)]
            c = copy(
                piece, back.at[me], fin_s.at[phase, o], fin_r.at[me], device(xx, z, phase)
            )
            if o:
                start(c)
            else:
                @pl.when(core != phase)
                def _():
                    c.start()

                @pl.when(core == phase)
                def _():
                    back[me] = tot[phase, my_rows, :]

    def wgrad(first, count):
        @pl.loop(first, first + count)
        def _(t):
            q = lax.div(t, quarter // 256)
            cols = pl.ds(pl.multiple_of(lax.rem(t, quarter // 256) * 256, 256), 256)
            left = a_ref[q, :, :, :, cols].reshape(-1, 256)
            right = carried[...].reshape(-1, width)
            d = lax.dot_general(left, right, (((0,), (0,)), ((), ())), preferred_element_type=F32)
            rows = pl.ds(pl.multiple_of(t * 256, 256), 256)
            wg[rows, :] = d.astype(BF)

            @pl.when(leading)
            def _():
                fold = jnp.zeros((256, 128), F32)
                for m in range(width // 128):
                    lanes = slice(m * 128, (m + 1) * 128)
                    fold += d[:, lanes] * w_ref[rows, lanes].astype(F32)
                line = jnp.sum(fold.T, axis=0, keepdims=True)
                gains = vec_ref[:, pl.ds(pl.multiple_of(rep * half_model + t * 256, 256), 256)]
                v_out[0, :, rows] = line / gains

        rows = pl.ds(first * 256, count * 256)
        c = pltpu.make_async_copy(wg.at[rows], grad_hbm.at[rows], wg_sem.at[len(copies)])
        c.start()
        copies.append(c)

    def vec_copy(t):
        return copy(v_out.at[t], v_in.at[t], v_s.at[t], v_r.at[t], doubling[t])

    def vec_next(t):
        vec_copy(t).wait_recv()
        v_out[t + 1] = v_out[t] + v_in[t]
        start(vec_copy(t + 1))

    half_model = model // 2
    copies = []

    for phase in (0, 1):
        group_wait(phase)
        ag_send(phase, UP, 0)
        ag_send(phase, DOWN, 0)
        sib_send(phase, 0)
    w_copy.wait()
    mm1(0)
    for u in range(1, 8):
        if u < 7:
            forward((u - 1) % 2, (u + 1) // 2)
        else:
            forward(0, 4)
            forward(1, 4)
        mm1(u)
        if u >= 2:
            mid1(u - 2)
        if u >= 4:
            mid2(u - 4)
        if u >= 5:
            mm2(u - 5)
    mid2(4)
    mid1(6)
    mid2(5)
    mm2(5)
    rs_step(0, DOWN, 0)
    mid1(7)
    mid2(6)
    mm2(6)
    rs_step(1, UP, 0)
    mm2(3)
    rs_step(0, DOWN, 1)
    mid2(7)
    mm2(7)
    rs_step(0, UP, 0)
    rs_step(1, DOWN, 0)
    mm2(4)
    rs_step(1, UP, 1)
    rs_step(0, DOWN, 2)
    rs_step(1, UP, 2)
    per = model // 512 // 3
    for i in range(1, 4):
        wgrad((i - 1) * per, per)
        rs_step(0, UP, i)
        rs_step(1, DOWN, i)

    @pl.when(jnp.logical_not(leading))
    def _():
        for q in range(2):
            line = jnp.zeros((1, quarter), F32)
            for xx in (xlo, xlo + 2):
                rows = pl.ds(pl.multiple_of(xx * 16, 16), 16)
                line += jnp.sum(a_ref[q, core, z, rows].astype(F32), axis=0, keepdims=True)
            v_out[0, :, q * quarter:(q + 1) * quarter] = line

    start(vec_copy(0))
    vec_next(0)
    rs_final(0)
    rs_final(1)
    vec_next(1)
    vec_next(2)

    copy(rows_ref, resid, resid_sem.at[0], resid_sem.at[1], sec_mate).wait_recv()
    for o in range(1, 8):
        j = lax.rem(me + o, 8)
        copy(back.at[j], back.at[j], fin_s.at[0, 0], fin_r.at[j], member(j)).wait_recv()

    def quarter_sum(q):
        j = (q // 2) * 4 + q % 2
        return back[j].astype(F32) + back[j + 2].astype(F32)

    @pl.when(leading)
    def _():
        mean = jnp.zeros((16, 1), F32)
        mix = jnp.zeros((16, 1), F32)
        for q in range(4):
            cols = slice(q * quarter, (q + 1) * quarter)
            s = quarter_sum(q)
            std = standard[:, cols]
            g = s * vec_ref[:, cols]
            summed[:, cols] = g
            mean += jnp.sum(g, axis=1, keepdims=True)
            mix += jnp.sum(g * std, axis=1, keepdims=True)
        mean = mean / model
        mix = mix / model
        rs = scale[:, 0:1]
        for q in range(4):
            cols = slice(q * quarter, (q + 1) * quarter)
            through = (summed[:, cols] - mean - standard[:, cols] * mix) * rs
            leave_ref[:, cols] = (resid[:, cols].astype(F32) + through).astype(BF)

    @pl.when(jnp.logical_not(leading))
    def _():
        for q in range(4):
            cols = slice(q * quarter, (q + 1) * quarter)
            leave_ref[:, cols] = (resid[:, cols].astype(F32) + quarter_sum(q) + vec_ref[:, cols]).astype(BF)

    vec_next(3)
    vec_next(4)
    vec_copy(5).wait_recv()
    mine = pl.ds(pl.multiple_of(rep * half_model, 128), half_model)
    other = pl.ds(pl.multiple_of((1 - rep) * half_model, 128), half_model)
    total_ref[:, mine] = v_out[5]
    total_ref[:, other] = v_in[5]

    for c in sent:
        c.wait_send()
    for phase in (0, 1):
        @pl.when(core != phase)
        def _():
            copy(
                tot.at[phase, my_rows], back.at[me], fin_s.at[phase, 0], fin_r.at[me], device(x, z, phase)
            ).wait_send()
    for c in copies:
        c.wait()


def local(weights, arriving, vectors):
    _, half, width = weights.shape
    _, micro, rows, model = arriving.shape
    quarter = model // 4
    dma = pltpu.SemaphoreType.DMA
    vm = pltpu.VMEM
    block = (64, quarter)
    leaving, weight_grad, totals = pl.pallas_call(
        kernel,
        out_shape=(
            jax.ShapeDtypeStruct((micro * rows, model), BF),
            jax.ShapeDtypeStruct((half, width), BF),
            jax.ShapeDtypeStruct((1, model), F32),
        ),
        in_specs=[
            pl.BlockSpec(memory_space=pl.ANY),
            pl.BlockSpec(memory_space=pltpu.VMEM),
            pl.BlockSpec(memory_space=pltpu.VMEM),
        ],
        out_specs=(
            pl.BlockSpec(memory_space=pltpu.VMEM),
            pl.BlockSpec(memory_space=pl.ANY),
            pl.BlockSpec(memory_space=pltpu.VMEM),
        ),
        scratch_shapes=[
            vm((half, width), BF),
            vm((4, 16, quarter), BF),
            vm((16, model), F32),
            vm((16, 128), F32),
            vm((16, model), BF),
            vm((2, 2, NZ, *block), BF),
            vm((8, 128, width), F32),
            vm((8, 128, width), BF),
            vm((8, 128, width), BF),
            vm((8, 128, width), BF),
            vm((8, 128, width), BF),
            vm((2, NZ, 64, width), BF),
            vm((2, NZ, *block), BF),
            vm((2, NZ, *block), BF),
            vm((2, NZ, *block), BF),
            vm((2, 2, 4, *block), BF),
            vm((half, width), BF),
            vm((2, *block), BF),
            vm((8, 16, quarter), BF),
            vm((16, model), F32),
            vm((6, 1, half), F32),
            vm((6, 1, half), F32),
            dma, dma((4,)), dma((8,)), dma((8,)), dma((2,)),
            dma((2, 2, 4)), dma((2, 2, 4)), dma((2, NZ)), dma((2, NZ)),
            dma((8,)), dma((8,)), dma((8,)), dma((8,)),
            dma((2, NZ)), dma((2, NZ)), dma((2, 2, 4)), dma((2, 2, 4)),
            dma((2, 4)), dma((8,)),
            dma((6,)), dma((6,)),
        ],
        compiler_params=pltpu.CompilerParams(
            collective_id=0, has_side_effects=True, vmem_limit_bytes=46 * 1024 * 1024
        ),
        cost_estimate=pl.CostEstimate(
            flops=3 * 2 * 1024 * half * width, bytes_accessed=4 * half * width, transcendentals=1024 * width
        ),
    )(weights[0], arriving[0].reshape(micro * rows, model), vectors)
    return (leaving.reshape(1, micro, rows, model), weight_grad[None], totals)


def solution(mesh):
    placed = (
        P("section", "dp", "tensor"),
        P("section", None, ("dp", "tensor"), None),
        P("section", None),
    )
    return jax.shard_map(
        local,
        mesh=mesh,
        in_specs=placed,
        out_specs=(
            P("section", None, ("dp", "tensor"), None),
            P("section", "dp", "tensor"),
            P("section", None),
        ),
        check_vma=False,
    )
```

```python
import functools

import jax
import jax.numpy as jnp
from jax import lax
from jax.experimental import pallas as pl
from jax.experimental.pallas import tpu as pltpu
from jax.sharding import PartitionSpec as P

coeff = 0.7978845608028654
BF = jnp.bfloat16
F32 = jnp.float32
NZ = 8
UP, DOWN = 0, 1


def steps_of(phase, way):
    return 4 if phase == way else 3


def kernel(
    weight_hbm, rows_ref, vec_ref,
    leave_ref, grad_hbm, total_ref,
    w_ref, stage, standard, scale, resid, a_ref,
    part, part_out, part_in, hid_out, hid_in, carried,
    y_own, y_out, y_in, x_out, x_in, ring_in, wg, tot, back, summed,
    v_out, v_in,
    w_sem, wg_sem, group_s, group_r, resid_sem, ag_s, ag_r, sib_s, sib_r,
    dp_s, dp_r, sec_s, sec_r, share_s, share_r, y_s, y_r, x_s, x_r, rs_s, rs_r, fin_s, fin_r,
    v_s, v_r,
):
    sec = lax.axis_index("section")
    rep = lax.axis_index("dp")
    ten = lax.axis_index("tensor")
    core = lax.rem(ten, 2)
    z = lax.rem(lax.div(ten, 2), NZ)
    xlo = lax.div(ten, 2 * NZ)
    x = rep * 2 + xlo
    me = x * 2 + core
    leading = lax.rem(sec, 2) == 0
    model = rows_ref.shape[1]
    quarter = model // 4
    width = w_ref.shape[1]
    partner_sec = sec + 1 - 2 * lax.rem(sec, 2)

    def device(xx, zz, cc):
        return (sec, lax.div(xx, 2), (lax.rem(xx, 2) * NZ + zz) * 2 + cc)

    def member(j):
        return device(lax.div(j, 2), z, lax.rem(j, 2))

    above = device(x, lax.rem(z + 1, NZ), core)
    below = device(x, lax.rem(z + NZ - 1, NZ), core)
    sibling = device(x, z, 1 - core)
    dp_mate = (sec, 1 - rep, ten)
    sec_mate = (partner_sec, rep, ten)

    def copy(src, dst, send, recv, target):
        return pltpu.make_async_remote_copy(
            src_ref=src, dst_ref=dst, send_sem=send, recv_sem=recv,
            device_id=target, device_id_type=pl.DeviceIdType.MESH,
        )

    def zblock(o):
        return lax.rem(z + o, NZ)

    sent = []

    def start(c):
        c.start()
        sent.append(c)

    barrier = pltpu.get_barrier_semaphore()
    friends = [member(lax.rem(me + o, 8)) for o in range(1, 8)]
    z2 = z + 2 - 4 * lax.rem(lax.div(z, 2), 2)
    doubling = [
        sibling, device(rep * 2 + 1 - xlo, z, core), device(x, z + 1 - 2 * lax.rem(z, 2), core),
        device(x, z2, core), device(x, zblock(4), core), dp_mate,
    ]
    friends += [above, below, doubling[3], doubling[4], sec_mate]
    for f in friends:
        pl.semaphore_signal(barrier, inc=1, device_id=f, device_id_type=pl.DeviceIdType.MESH)
    w_copy = pltpu.make_async_copy(weight_hbm, w_ref, w_sem)
    w_copy.start()

    @pl.when(leading)
    def _():
        acc = jnp.zeros((16, 1), F32)
        for q in range(4):
            acc += jnp.sum(rows_ref[:, q * quarter:(q + 1) * quarter].astype(F32), axis=1, keepdims=True)
        mean = acc / model
        acc = jnp.zeros((16, 1), F32)
        for q in range(4):
            cen = rows_ref[:, q * quarter:(q + 1) * quarter].astype(F32) - mean
            acc += jnp.sum(cen * cen, axis=1, keepdims=True)
        rs = lax.rsqrt(acc / model + 1e-05)
        scale[...] = jnp.broadcast_to(rs, scale.shape)
        for q in range(4):
            cols = slice(q * quarter, (q + 1) * quarter)
            std = (rows_ref[:, cols].astype(F32) - mean) * rs
            standard[:, cols] = std
            stage[q] = (std * vec_ref[:, cols]).astype(BF)

    @pl.when(jnp.logical_not(leading))
    def _():
        for q in range(4):
            stage[q] = rows_ref[:, q * quarter:(q + 1) * quarter]

    pl.semaphore_wait(barrier, len(friends))

    my_rows = pl.ds(pl.multiple_of(x * 16, 16), 16)
    for o in range(1, 8):
        j = lax.rem(me + o, 8)
        q = lax.div(j, 4) * 2 + lax.rem(j, 2)
        start(copy(
            stage.at[q], a_ref.at[lax.rem(j, 2), core, z, my_rows],
            group_s.at[o], group_r.at[me], member(j),
        ))
    a_ref[core, core, z, my_rows] = stage[rep * 2 + core]
    start(copy(rows_ref, resid, resid_sem.at[0], resid_sem.at[1], sec_mate))

    def group_wait(phase):
        for o in range(4):
            xx = lax.rem(x + o, 4)
            piece = a_ref.at[core, phase, z, pl.ds(pl.multiple_of(xx * 16, 16), 16)]
            sender = xx * 2 + phase

            def wait():
                copy(piece, piece, group_s.at[0], group_r.at[sender], member(sender)).wait_recv()

            if o:
                wait()
            else:
                pl.when(core != phase)(wait)

    def ag_send(phase, way, k):
        o = (NZ - k) % NZ if way == UP else k
        block = a_ref.at[core, phase, zblock(o)]
        start(copy(
            block, block, ag_s.at[phase, way, k], ag_r.at[phase, way, k],
            above if way == UP else below,
        ))

    def ag_wait(phase, way, k):
        o = NZ - 1 - k if way == UP else k + 1
        block = a_ref.at[core, phase, zblock(o)]
        copy(
            block, block, ag_s.at[phase, way, k], ag_r.at[phase, way, k],
            above if way == UP else below,
        ).wait_recv()
        return o

    def sib_send(phase, o):
        block = a_ref.at[core, phase, zblock(o)]
        start(copy(block, block, sib_s.at[phase, o], sib_r.at[phase, o], sibling))

    def sib_wait(phase, o):
        block = a_ref.at[1 - core, phase, zblock(o)]
        copy(block, block, sib_s.at[phase, o], sib_r.at[phase, o], sibling).wait_recv()

    def forward(phase, j):
        for way in (UP, DOWN):
            count = steps_of(phase, way)
            if j > count:
                continue
            o = ag_wait(phase, way, j - 1)
            if j < count:
                ag_send(phase, way, j)
            sib_send(phase, o)

    units = [((0, 0), (1, 0))]
    for k in (1, 2, 3):
        units += [((phase, NZ - k), (phase, k)) for phase in (0, 1)]
    units += [((0, 4), (1, 4))]

    def blocks_of(group):
        return [(phase, o, zblock(o)) for u in group for phase, o in units[u]]

    def mm1(*group):
        blocks = blocks_of(group)
        for phase, o, _ in blocks:
            sib_wait(phase, o)

        @pl.loop(0, width // 256)
        def _(n):
            cols = pl.ds(pl.multiple_of(n * 256, 256), 256)
            acc = None
            for q in range(2):
                left = jnp.concatenate([a_ref[q, phase, b] for phase, _, b in blocks], axis=0)
                d = jnp.dot(left, w_ref[q * quarter:(q + 1) * quarter, cols], preferred_element_type=F32)
                acc = d if acc is None else acc + d
            for i, u in enumerate(group):
                part[u, :, cols] = acc[i * 128:(i + 1) * 128]
                part_out[u, :, cols] = acc[i * 128:(i + 1) * 128].astype(BF)

        for u in group:
            start(dp_copy(u))

    def dp_copy(u):
        theirs = pl.ds(pl.multiple_of((1 - rep) * 64, 64), 64)
        return copy(part_out.at[u, theirs], part_in.at[u], dp_s.at[u], dp_r.at[u], dp_mate)

    def sec_copy(u):
        return copy(hid_out.at[u], hid_in.at[u], sec_s.at[u], sec_r.at[u], sec_mate)

    def own_block(u):
        (p1, o1), (p2, o2) = units[u]
        return p1 + rep * (p2 - p1), zblock(o1 + rep * (o2 - o1))

    def share_copy(u):
        phase, b = own_block(u)
        block = carried.at[phase, b]
        return copy(block, block, share_s.at[u], share_r.at[u], dp_mate)

    def mid1(u):
        dp_copy(u).wait_recv()

        @pl.when(leading)
        def _():
            @pl.loop(0, 4)
            def _(n):
                rows = pl.ds(pl.multiple_of(n * 16, 16), 16)
                mine = pl.ds(pl.multiple_of(rep * 64 + n * 16, 16), 16)
                p = part[u, mine, :] + part_in[u, rows, :].astype(F32)
                sq = p * p
                inner = jnp.tanh(coeff * (p + 0.044715 * sq * p))
                one = 1.0 + inner
                hid_out[u, rows, :] = (0.5 * p * one).astype(BF)
                part[u, mine, :] = 0.5 * one + 0.5 * p * (1.0 - inner * inner) * coeff * (
                    1.0 + 3.0 * 0.044715 * sq
                )

        @pl.when(jnp.logical_not(leading))
        def _():
            @pl.loop(0, 4)
            def _(n):
                rows = pl.ds(pl.multiple_of(n * 16, 16), 16)
                mine = pl.ds(pl.multiple_of(rep * 64 + n * 16, 16), 16)
                hid_out[u, rows, :] = (part[u, mine, :] + part_in[u, rows, :].astype(F32)).astype(BF)

        start(sec_copy(u))

    def mid2(u):
        sec_copy(u).wait_recv()
        phase, b = own_block(u)

        @pl.when(leading)
        def _():
            @pl.loop(0, 4)
            def _(n):
                rows = pl.ds(pl.multiple_of(n * 16, 16), 16)
                mine = pl.ds(pl.multiple_of(rep * 64 + n * 16, 16), 16)
                carried[phase, b, rows, :] = (hid_in[u, rows, :].astype(F32) * part[u, mine, :]).astype(BF)

        @pl.when(jnp.logical_not(leading))
        def _():
            carried[phase, b] = hid_in[u]

        start(share_copy(u))

    def mm2(*group):
        for u in group:
            share_copy(u).wait_recv()
        blocks = blocks_of(group)
        for half, dst in ((1 - core, y_out), (core, y_own)):
            @pl.loop(0, quarter // 256)
            def _(n):
                left = jnp.concatenate([carried[phase, b] for phase, _, b in blocks], axis=0)
                right = w_ref[pl.ds(pl.multiple_of(half * quarter + n * 256, 256), 256), :]
                d = lax.dot_general(left, right, (((1,), (1,)), ((), ())), preferred_element_type=F32)
                cols = pl.ds(pl.multiple_of(n * 256, 256), 256)
                for i, (phase, o, _) in enumerate(blocks):
                    dst[phase, o, :, cols] = d[i * 64:(i + 1) * 64].astype(BF)

                @pl.when(leading)
                def _():
                    line = None
                    for i, (phase, _, b) in enumerate(blocks):
                        term = d[i * 64:(i + 1) * 64] * a_ref[half, phase, b, :, cols].astype(F32)
                        line = term if line is None else line + term
                    line = jnp.sum(line, axis=0, keepdims=True)
                    place = pl.ds(pl.multiple_of(half * quarter + n * 256, 256), 256)
                    v_out[0, :, place] = line if group[0] == 0 else v_out[0, :, place] + line

            if dst is y_out:
                for phase, o, _ in blocks:
                    start(copy(
                        y_out.at[phase, o], y_in.at[phase, o], y_s.at[phase, o], y_r.at[phase, o], sibling
                    ))

    def y_wait(phase, o):
        copy(
            y_out.at[phase, o], y_in.at[phase, o], y_s.at[phase, o], y_r.at[phase, o], sibling
        ).wait_recv()

    third = quarter // 3
    both = slice(0, third)
    mine_to = slice(third, 2 * third)
    mine_cols = pl.ds(pl.multiple_of(third + xlo * third, 128), third)
    theirs_cols = pl.ds(pl.multiple_of(2 * third - xlo * third, 128), third)
    ring_cols = slice(0, 2 * third)

    def x_copy(phase, o):
        return copy(x_out.at[phase, o], x_in.at[phase, o], x_s.at[phase, o], x_r.at[phase, o], doubling[1])

    def x_step(phase, o):
        y_wait(phase, o)

        @pl.loop(0, 4)
        def _(n):
            rows = pl.ds(pl.multiple_of(n * 16, 16), 16)
            x_out[phase, o, rows, :] = (
                y_own[phase, o, rows, theirs_cols].astype(F32) + y_in[phase, o, rows, theirs_cols].astype(F32)
            ).astype(BF)

        start(x_copy(phase, o))

    def block_sums(phase, o, rows):
        common = y_own[phase, o, rows, both].astype(F32) + y_in[phase, o, rows, both].astype(F32)
        own = y_own[phase, o, rows, mine_cols].astype(F32) + y_in[phase, o, rows, mine_cols].astype(F32)
        return common, own + x_in[phase, o, rows, :].astype(F32)

    def rs_copy(phase, way, i):
        count = steps_of(phase, way)
        o = count - i if way == UP else NZ - (count - i)
        return o, copy(
            y_own.at[phase, o, :, ring_cols], ring_in.at[phase, way, i],
            rs_s.at[phase, way, i], rs_r.at[phase, way, i],
            above if way == UP else below,
        )

    def rs_step(phase, way, i):
        o, c = rs_copy(phase, way, i)
        x_copy(phase, o).wait_recv()
        if i:
            rs_copy(phase, way, i - 1)[1].wait_recv()

        @pl.loop(0, 4)
        def _(n):
            rows = pl.ds(pl.multiple_of(n * 16, 16), 16)
            common, own = block_sums(phase, o, rows)
            if i:
                common += ring_in[phase, way, i - 1, rows, both].astype(F32)
                own += ring_in[phase, way, i - 1, rows, mine_to].astype(F32)
            y_own[phase, o, rows, both] = common.astype(BF)
            y_own[phase, o, rows, mine_to] = own.astype(BF)

        start(c)

    def rs_final(phase):
        x_copy(phase, 0).wait_recv()
        last = [steps_of(phase, way) - 1 for way in (UP, DOWN)]
        for way in (UP, DOWN):
            rs_copy(phase, way, last[way])[1].wait_recv()

        @pl.loop(0, 4)
        def _(n):
            rows = pl.ds(pl.multiple_of(n * 16, 16), 16)
            common, own = block_sums(phase, 0, rows)
            for way in (UP, DOWN):
                common += ring_in[phase, way, last[way], rows, both].astype(F32)
                own += ring_in[phase, way, last[way], rows, mine_to].astype(F32)
            tot[phase, rows, both] = common.astype(BF)
            tot[phase, rows, mine_to] = own.astype(BF)

        for o in range(4):
            xx = lax.rem(x + o, 4)
            piece = tot.at[phase, pl.ds(pl.multiple_of(xx * 16, 16), 16)]
            c = copy(
                piece, back.at[me], fin_s.at[phase, o], fin_r.at[me], device(xx, z, phase)
            )
            if o:
                start(c)
            else:
                @pl.when(core != phase)
                def _():
                    c.start()

                @pl.when(core == phase)
                def _():
                    back[me] = tot[phase, my_rows, :]

    def wgrad(first, count):
        @pl.loop(first, first + count)
        def _(t):
            q = lax.div(t, quarter // 256)
            cols = pl.ds(pl.multiple_of(lax.rem(t, quarter // 256) * 256, 256), 256)
            left = a_ref[q, :, :, :, cols].reshape(-1, 256)
            right = carried[...].reshape(-1, width)
            d = lax.dot_general(left, right, (((0,), (0,)), ((), ())), preferred_element_type=F32)
            rows = pl.ds(pl.multiple_of(t * 256, 256), 256)
            wg[rows, :] = d.astype(BF)

        rows = pl.ds(first * 256, count * 256)
        c = pltpu.make_async_copy(wg.at[rows], grad_hbm.at[rows], wg_sem.at[len(copies)])
        c.start()
        copies.append(c)

    def vec_copy(t):
        return copy(v_out.at[t], v_in.at[t], v_s.at[t], v_r.at[t], doubling[t])

    def vec_next(t):
        vec_copy(t).wait_recv()
        v_out[t + 1] = v_out[t] + v_in[t]
        start(vec_copy(t + 1))

    half_model = model // 2
    copies = []

    for phase in (0, 1):
        group_wait(phase)
        ag_send(phase, UP, 0)
        ag_send(phase, DOWN, 0)
        sib_send(phase, 0)
    w_copy.wait()
    mm1(0)
    for j in range(1, 5):
        forward(0, j)
        forward(1, j)
        if j == 1:
            mm1(1, 2)
            mid1(0)
        elif j == 2:
            mm1(3, 4)
            mid2(0)
            mid1(1)
            mid1(2)
        elif j == 3:
            mm1(5, 6)
            mid2(1)
            mid2(2)
            mid1(3)
            mid1(4)
            mm2(0)
        else:
            mm1(7)
            mid2(3)
            mid2(4)
            mid1(5)
            mid1(6)
            mm2(1, 2)
    mid1(7)
    mid2(5)
    mid2(6)
    mm2(3, 4)
    mid2(7)
    mm2(5, 6)
    x_step(0, 5)
    x_step(1, 3)
    mm2(7)

    @pl.when(leading)
    def _():
        gains = vec_ref[:, pl.ds(pl.multiple_of(rep * half_model, 128), half_model)]
        v_out[0] = v_out[0] / gains

    @pl.when(jnp.logical_not(leading))
    def _():
        for q in range(2):
            line = jnp.zeros((1, quarter), F32)
            for xx in (xlo, xlo + 2):
                rows = pl.ds(pl.multiple_of(xx * 16, 16), 16)
                line += jnp.sum(a_ref[q, core, z, rows].astype(F32), axis=0, keepdims=True)
            v_out[0, :, q * quarter:(q + 1) * quarter] = line

    start(vec_copy(0))
    x_step(0, 4)
    x_step(1, 4)
    rs_step(0, DOWN, 0)
    rs_step(1, UP, 0)
    vec_next(0)
    x_step(0, 6)
    x_step(1, 2)
    rs_step(0, UP, 0)
    rs_step(1, DOWN, 0)
    x_step(0, 3)
    x_step(1, 5)
    rs_step(0, DOWN, 1)
    rs_step(1, UP, 1)
    vec_next(1)
    x_step(0, 7)
    x_step(1, 1)
    wgrad(0, 2)
    rs_step(0, UP, 1)
    rs_step(1, DOWN, 1)
    x_step(0, 2)
    x_step(1, 6)
    rs_step(0, DOWN, 2)
    rs_step(1, UP, 2)
    vec_next(2)
    x_step(0, 1)
    x_step(1, 7)
    wgrad(2, 2)
    rs_step(0, UP, 2)
    rs_step(1, DOWN, 2)
    vec_next(3)
    x_step(0, 0)
    x_step(1, 0)
    wgrad(4, 2)
    rs_step(0, UP, 3)
    rs_step(1, DOWN, 3)
    vec_next(4)
    wgrad(6, 3)
    rs_final(0)
    rs_final(1)
    wgrad(9, 3)

    copy(rows_ref, resid, resid_sem.at[0], resid_sem.at[1], sec_mate).wait_recv()
    for o in range(1, 8):
        j = lax.rem(me + o, 8)
        copy(back.at[j], back.at[j], fin_s.at[0, 0], fin_r.at[j], member(j)).wait_recv()

    def quarter_sum(q):
        j = (q // 2) * 4 + q % 2
        return jnp.concatenate([
            back[j, :, both].astype(F32) + back[j + 2, :, both].astype(F32),
            back[j, :, mine_to].astype(F32),
            back[j + 2, :, mine_to].astype(F32),
        ], axis=1)

    @pl.when(leading)
    def _():
        mean = jnp.zeros((16, 1), F32)
        mix = jnp.zeros((16, 1), F32)
        for q in range(4):
            cols = slice(q * quarter, (q + 1) * quarter)
            s = quarter_sum(q)
            std = standard[:, cols]
            g = s * vec_ref[:, cols]
            summed[:, cols] = g
            mean += jnp.sum(g, axis=1, keepdims=True)
            mix += jnp.sum(g * std, axis=1, keepdims=True)
        mean = mean / model
        mix = mix / model
        rs = scale[:, 0:1]
        for q in range(4):
            cols = slice(q * quarter, (q + 1) * quarter)
            through = (summed[:, cols] - mean - standard[:, cols] * mix) * rs
            leave_ref[:, cols] = (resid[:, cols].astype(F32) + through).astype(BF)

    @pl.when(jnp.logical_not(leading))
    def _():
        for q in range(4):
            cols = slice(q * quarter, (q + 1) * quarter)
            leave_ref[:, cols] = (resid[:, cols].astype(F32) + quarter_sum(q) + vec_ref[:, cols]).astype(BF)

    vec_copy(5).wait_recv()
    mine = pl.ds(pl.multiple_of(rep * half_model, 128), half_model)
    other = pl.ds(pl.multiple_of((1 - rep) * half_model, 128), half_model)
    total_ref[:, mine] = v_out[5]
    total_ref[:, other] = v_in[5]

    for c in sent:
        c.wait_send()
    for phase in (0, 1):
        @pl.when(core != phase)
        def _():
            copy(
                tot.at[phase, my_rows], back.at[me], fin_s.at[phase, 0], fin_r.at[me], device(x, z, phase)
            ).wait_send()
    for c in copies:
        c.wait()


def local(weights, arriving, vectors):
    _, half, width = weights.shape
    _, micro, rows, model = arriving.shape
    quarter = model // 4
    dma = pltpu.SemaphoreType.DMA
    vm = pltpu.VMEM
    block = (64, quarter)
    third = quarter // 3
    leaving, weight_grad, totals = pl.pallas_call(
        kernel,
        out_shape=(
            jax.ShapeDtypeStruct((micro * rows, model), BF),
            jax.ShapeDtypeStruct((half, width), BF),
            jax.ShapeDtypeStruct((1, model), F32),
        ),
        in_specs=[
            pl.BlockSpec(memory_space=pl.ANY),
            pl.BlockSpec(memory_space=pltpu.VMEM),
            pl.BlockSpec(memory_space=pltpu.VMEM),
        ],
        out_specs=(
            pl.BlockSpec(memory_space=pltpu.VMEM),
            pl.BlockSpec(memory_space=pl.ANY),
            pl.BlockSpec(memory_space=pltpu.VMEM),
        ),
        scratch_shapes=[
            vm((half, width), BF),
            vm((4, 16, quarter), BF),
            vm((16, model), F32),
            vm((16, 128), F32),
            vm((16, model), BF),
            vm((2, 2, NZ, *block), BF),
            vm((8, 128, width), F32),
            vm((8, 128, width), BF),
            vm((8, 64, width), BF),
            vm((8, 64, width), BF),
            vm((8, 64, width), BF),
            vm((2, NZ, 64, width), BF),
            vm((2, NZ, *block), BF),
            vm((2, NZ, *block), BF),
            vm((2, NZ, *block), BF),
            vm((2, NZ, 64, third), BF),
            vm((2, NZ, 64, third), BF),
            vm((2, 2, 4, 64, 2 * third), BF),
            vm((half, width), BF),
            vm((2, 64, 2 * third), BF),
            vm((8, 16, 2 * third), BF),
            vm((16, model), F32),
            vm((6, 1, half), F32),
            vm((6, 1, half), F32),
            dma, dma((5,)), dma((8,)), dma((8,)), dma((2,)),
            dma((2, 2, 4)), dma((2, 2, 4)), dma((2, NZ)), dma((2, NZ)),
            dma((8,)), dma((8,)), dma((8,)), dma((8,)), dma((8,)), dma((8,)),
            dma((2, NZ)), dma((2, NZ)), dma((2, NZ)), dma((2, NZ)), dma((2, 2, 4)), dma((2, 2, 4)),
            dma((2, 4)), dma((8,)),
            dma((6,)), dma((6,)),
        ],
        compiler_params=pltpu.CompilerParams(
            collective_id=0, has_side_effects=True, vmem_limit_bytes=46 * 1024 * 1024
        ),
        cost_estimate=pl.CostEstimate(
            flops=3 * 2 * 1024 * half * width, bytes_accessed=4 * half * width, transcendentals=1024 * width
        ),
    )(weights[0], arriving[0].reshape(micro * rows, model), vectors)
    return (leaving.reshape(1, micro, rows, model), weight_grad[None], totals)


def solution(mesh):
    placed = (
        P("section", "dp", "tensor"),
        P("section", None, ("dp", "tensor"), None),
        P("section", None),
    )
    return jax.shard_map(
        local,
        mesh=mesh,
        in_specs=placed,
        out_specs=(
            P("section", None, ("dp", "tensor"), None),
            P("section", "dp", "tensor"),
            P("section", None),
        ),
        check_vma=False,
    )
```

```python
import functools

import jax
import jax.numpy as jnp
from jax import lax
from jax.experimental import pallas as pl
from jax.experimental.pallas import tpu as pltpu
from jax.sharding import PartitionSpec as P

coeff = 0.7978845608028654
BF = jnp.bfloat16
F32 = jnp.float32
NZ = 8
UP, DOWN = 0, 1


def steps_of(phase, way):
    return 4 if phase == way else 3


def kernel(
    weight_hbm, rows_ref, vec_ref,
    leave_ref, grad_hbm, total_ref,
    w_ref, stage, standard, scale, resid, a_ref,
    part, part_out, part_in, hid_out, hid_in, carried,
    y_own, y_out, y_in, x_out, x_in, ring_in, wg, tot, back, summed,
    v_out, v_in,
    w_sem, wg_sem, group_s, group_r, resid_sem, ag_s, ag_r, sib_s, sib_r,
    dp_s, dp_r, sec_s, sec_r, share_s, share_r, y_s, y_r, x_s, x_r, rs_s, rs_r, fin_s, fin_r,
    v_s, v_r,
):
    sec = lax.axis_index("section")
    rep = lax.axis_index("dp")
    ten = lax.axis_index("tensor")
    core = lax.rem(ten, 2)
    z = lax.rem(lax.div(ten, 2), NZ)
    xlo = lax.div(ten, 2 * NZ)
    x = rep * 2 + xlo
    me = x * 2 + core
    leading = lax.rem(sec, 2) == 0
    model = rows_ref.shape[1]
    quarter = model // 4
    width = w_ref.shape[1]
    partner_sec = sec + 1 - 2 * lax.rem(sec, 2)

    def device(xx, zz, cc):
        return (sec, lax.div(xx, 2), (lax.rem(xx, 2) * NZ + zz) * 2 + cc)

    def member(j):
        return device(lax.div(j, 2), z, lax.rem(j, 2))

    above = device(x, lax.rem(z + 1, NZ), core)
    below = device(x, lax.rem(z + NZ - 1, NZ), core)
    sibling = device(x, z, 1 - core)
    dp_mate = (sec, 1 - rep, ten)
    sec_mate = (partner_sec, rep, ten)

    def copy(src, dst, send, recv, target):
        return pltpu.make_async_remote_copy(
            src_ref=src, dst_ref=dst, send_sem=send, recv_sem=recv,
            device_id=target, device_id_type=pl.DeviceIdType.MESH,
        )

    def zblock(o):
        return lax.rem(z + o, NZ)

    sent = []

    def start(c):
        c.start()
        sent.append(c)

    barrier = pltpu.get_barrier_semaphore()
    friends = [member(lax.rem(me + o, 8)) for o in range(1, 8)]
    z2 = z + 2 - 4 * lax.rem(lax.div(z, 2), 2)
    doubling = [
        sibling, device(rep * 2 + 1 - xlo, z, core), device(x, z + 1 - 2 * lax.rem(z, 2), core),
        device(x, z2, core), device(x, zblock(4), core), dp_mate,
    ]
    friends += [above, below, doubling[3], doubling[4], sec_mate]
    for f in friends:
        pl.semaphore_signal(barrier, inc=1, device_id=f, device_id_type=pl.DeviceIdType.MESH)
    w_copy = pltpu.make_async_copy(weight_hbm, w_ref, w_sem)
    w_copy.start()

    @pl.when(leading)
    def _():
        acc = jnp.zeros((16, 1), F32)
        for q in range(4):
            acc += jnp.sum(rows_ref[:, q * quarter:(q + 1) * quarter].astype(F32), axis=1, keepdims=True)
        mean = acc / model
        acc = jnp.zeros((16, 1), F32)
        for q in range(4):
            cen = rows_ref[:, q * quarter:(q + 1) * quarter].astype(F32) - mean
            acc += jnp.sum(cen * cen, axis=1, keepdims=True)
        rs = lax.rsqrt(acc / model + 1e-05)
        scale[...] = jnp.broadcast_to(rs, scale.shape)
        for q in range(4):
            cols = slice(q * quarter, (q + 1) * quarter)
            std = (rows_ref[:, cols].astype(F32) - mean) * rs
            standard[:, cols] = std
            stage[q] = (std * vec_ref[:, cols]).astype(BF)

    @pl.when(jnp.logical_not(leading))
    def _():
        for q in range(4):
            stage[q] = rows_ref[:, q * quarter:(q + 1) * quarter]

    pl.semaphore_wait(barrier, len(friends))

    my_rows = pl.ds(pl.multiple_of(x * 16, 16), 16)
    for o in range(1, 8):
        j = lax.rem(me + o, 8)
        q = lax.div(j, 4) * 2 + lax.rem(j, 2)
        start(copy(
            stage.at[q], a_ref.at[lax.rem(j, 2), core, z, my_rows],
            group_s.at[o], group_r.at[me], member(j),
        ))
    a_ref[core, core, z, my_rows] = stage[rep * 2 + core]
    start(copy(rows_ref, resid, resid_sem.at[0], resid_sem.at[1], sec_mate))

    def group_wait(phase):
        for o in range(4):
            xx = lax.rem(x + o, 4)
            piece = a_ref.at[core, phase, z, pl.ds(pl.multiple_of(xx * 16, 16), 16)]
            sender = xx * 2 + phase

            def wait():
                copy(piece, piece, group_s.at[0], group_r.at[sender], member(sender)).wait_recv()

            if o:
                wait()
            else:
                pl.when(core != phase)(wait)

    def ag_send(phase, way, k):
        o = (NZ - k) % NZ if way == UP else k
        block = a_ref.at[core, phase, zblock(o)]
        start(copy(
            block, block, ag_s.at[phase, way, k], ag_r.at[phase, way, k],
            above if way == UP else below,
        ))

    def ag_wait(phase, way, k):
        o = NZ - 1 - k if way == UP else k + 1
        block = a_ref.at[core, phase, zblock(o)]
        copy(
            block, block, ag_s.at[phase, way, k], ag_r.at[phase, way, k],
            above if way == UP else below,
        ).wait_recv()
        return o

    def sib_send(phase, o):
        block = a_ref.at[core, phase, zblock(o)]
        start(copy(block, block, sib_s.at[phase, o], sib_r.at[phase, o], sibling))

    def sib_wait(phase, o):
        block = a_ref.at[1 - core, phase, zblock(o)]
        copy(block, block, sib_s.at[phase, o], sib_r.at[phase, o], sibling).wait_recv()

    def forward(phase, j):
        for way in (UP, DOWN):
            count = steps_of(phase, way)
            if j > count:
                continue
            o = ag_wait(phase, way, j - 1)
            if j < count:
                ag_send(phase, way, j)
            sib_send(phase, o)

    units = [((0, 0), (1, 0))]
    for k in (1, 2, 3):
        units += [((phase, NZ - k), (phase, k)) for phase in (0, 1)]
    units += [((0, 4), (1, 4))]

    def blocks_of(group):
        return [(phase, o, zblock(o)) for u in group for phase, o in units[u]]

    def mm1(*group):
        blocks = blocks_of(group)
        for phase, o, _ in blocks:
            sib_wait(phase, o)

        @pl.loop(0, width // 256)
        def _(n):
            cols = pl.ds(pl.multiple_of(n * 256, 256), 256)
            acc = None
            for q in range(2):
                left = jnp.concatenate([a_ref[q, phase, b] for phase, _, b in blocks], axis=0)
                d = jnp.dot(left, w_ref[q * quarter:(q + 1) * quarter, cols], preferred_element_type=F32)
                acc = d if acc is None else acc + d
            for i, u in enumerate(group):
                part[u, :, cols] = acc[i * 128:(i + 1) * 128]
                part_out[u, :, cols] = acc[i * 128:(i + 1) * 128].astype(BF)

        for u in group:
            start(dp_copy(u))

    def dp_copy(u):
        theirs = pl.ds(pl.multiple_of((1 - rep) * 64, 64), 64)
        return copy(part_out.at[u, theirs], part_in.at[u], dp_s.at[u], dp_r.at[u], dp_mate)

    def sec_copy(u):
        return copy(hid_out.at[u], hid_in.at[u], sec_s.at[u], sec_r.at[u], sec_mate)

    def own_block(u):
        (p1, o1), (p2, o2) = units[u]
        return p1 + rep * (p2 - p1), zblock(o1 + rep * (o2 - o1))

    def share_copy(u):
        phase, b = own_block(u)
        block = carried.at[phase, b]
        return copy(block, block, share_s.at[u], share_r.at[u], dp_mate)

    def mid1(u):
        dp_copy(u).wait_recv()

        @pl.when(leading)
        def _():
            @pl.loop(0, 4)
            def _(n):
                rows = pl.ds(pl.multiple_of(n * 16, 16), 16)
                mine = pl.ds(pl.multiple_of(rep * 64 + n * 16, 16), 16)
                p = part[u, mine, :] + part_in[u, rows, :].astype(F32)
                sq = p * p
                inner = jnp.tanh(coeff * (p + 0.044715 * sq * p))
                one = 1.0 + inner
                hid_out[u, rows, :] = (0.5 * p * one).astype(BF)
                part[u, mine, :] = 0.5 * one + 0.5 * p * (1.0 - inner * inner) * coeff * (
                    1.0 + 3.0 * 0.044715 * sq
                )

        @pl.when(jnp.logical_not(leading))
        def _():
            @pl.loop(0, 4)
            def _(n):
                rows = pl.ds(pl.multiple_of(n * 16, 16), 16)
                mine = pl.ds(pl.multiple_of(rep * 64 + n * 16, 16), 16)
                hid_out[u, rows, :] = (part[u, mine, :] + part_in[u, rows, :].astype(F32)).astype(BF)

        start(sec_copy(u))

    def mid2(u):
        sec_copy(u).wait_recv()
        phase, b = own_block(u)

        @pl.when(leading)
        def _():
            @pl.loop(0, 4)
            def _(n):
                rows = pl.ds(pl.multiple_of(n * 16, 16), 16)
                mine = pl.ds(pl.multiple_of(rep * 64 + n * 16, 16), 16)
                carried[phase, b, rows, :] = (hid_in[u, rows, :].astype(F32) * part[u, mine, :]).astype(BF)

        @pl.when(jnp.logical_not(leading))
        def _():
            carried[phase, b] = hid_in[u]

        start(share_copy(u))

    def mm2(*group):
        for u in group:
            share_copy(u).wait_recv()
        blocks = blocks_of(group)
        for half, dst in ((1 - core, y_out), (core, y_own)):
            @pl.loop(0, quarter // 256)
            def _(n):
                left = jnp.concatenate([carried[phase, b] for phase, _, b in blocks], axis=0)
                right = w_ref[pl.ds(pl.multiple_of(half * quarter + n * 256, 256), 256), :]
                d = lax.dot_general(left, right, (((1,), (1,)), ((), ())), preferred_element_type=F32)
                cols = pl.ds(pl.multiple_of(n * 256, 256), 256)
                for i, (phase, o, _) in enumerate(blocks):
                    dst[phase, o, :, cols] = d[i * 64:(i + 1) * 64].astype(BF)

                @pl.when(leading)
                def _():
                    line = None
                    for i, (phase, _, b) in enumerate(blocks):
                        term = d[i * 64:(i + 1) * 64] * a_ref[half, phase, b, :, cols].astype(F32)
                        line = term if line is None else line + term
                    line = jnp.sum(line, axis=0, keepdims=True)
                    place = pl.ds(pl.multiple_of(half * quarter + n * 256, 256), 256)
                    v_out[0, :, place] = line if group[0] == 0 else v_out[0, :, place] + line

            if dst is y_out:
                for phase, o, _ in blocks:
                    start(copy(
                        y_out.at[phase, o], y_in.at[phase, o], y_s.at[phase, o], y_r.at[phase, o], sibling
                    ))

    def y_wait(phase, o):
        copy(
            y_out.at[phase, o], y_in.at[phase, o], y_s.at[phase, o], y_r.at[phase, o], sibling
        ).wait_recv()

    third = quarter // 3
    both = slice(0, third)
    mine_to = slice(third, 2 * third)
    mine_cols = pl.ds(pl.multiple_of(third + xlo * third, 128), third)
    theirs_cols = pl.ds(pl.multiple_of(2 * third - xlo * third, 128), third)
    ring_cols = slice(0, 2 * third)

    def x_copy(phase, o):
        return copy(x_out.at[phase, o], x_in.at[phase, o], x_s.at[phase, o], x_r.at[phase, o], doubling[1])

    def x_step(phase, o):
        y_wait(phase, o)

        @pl.loop(0, 4)
        def _(n):
            rows = pl.ds(pl.multiple_of(n * 16, 16), 16)
            x_out[phase, o, rows, :] = (
                y_own[phase, o, rows, theirs_cols].astype(F32) + y_in[phase, o, rows, theirs_cols].astype(F32)
            ).astype(BF)

        start(x_copy(phase, o))

    def block_sums(phase, o, rows):
        common = y_own[phase, o, rows, both].astype(F32) + y_in[phase, o, rows, both].astype(F32)
        own = y_own[phase, o, rows, mine_cols].astype(F32) + y_in[phase, o, rows, mine_cols].astype(F32)
        return common, own + x_in[phase, o, rows, :].astype(F32)

    def rs_copy(phase, way, i):
        count = steps_of(phase, way)
        o = count - i if way == UP else NZ - (count - i)
        return o, copy(
            y_own.at[phase, o, :, ring_cols], ring_in.at[phase, way, i],
            rs_s.at[phase, way, i], rs_r.at[phase, way, i],
            above if way == UP else below,
        )

    def rs_step(phase, way, i):
        o, c = rs_copy(phase, way, i)
        x_copy(phase, o).wait_recv()
        if i:
            rs_copy(phase, way, i - 1)[1].wait_recv()

        @pl.loop(0, 4)
        def _(n):
            rows = pl.ds(pl.multiple_of(n * 16, 16), 16)
            common, own = block_sums(phase, o, rows)
            if i:
                common += ring_in[phase, way, i - 1, rows, both].astype(F32)
                own += ring_in[phase, way, i - 1, rows, mine_to].astype(F32)
            y_own[phase, o, rows, both] = common.astype(BF)
            y_own[phase, o, rows, mine_to] = own.astype(BF)

        start(c)

    def rs_final(phase):
        x_copy(phase, 0).wait_recv()
        last = [steps_of(phase, way) - 1 for way in (UP, DOWN)]
        for way in (UP, DOWN):
            rs_copy(phase, way, last[way])[1].wait_recv()

        @pl.loop(0, 4)
        def _(n):
            rows = pl.ds(pl.multiple_of(n * 16, 16), 16)
            common, own = block_sums(phase, 0, rows)
            for way in (UP, DOWN):
                common += ring_in[phase, way, last[way], rows, both].astype(F32)
                own += ring_in[phase, way, last[way], rows, mine_to].astype(F32)
            tot[phase, rows, both] = common.astype(BF)
            tot[phase, rows, mine_to] = own.astype(BF)

        for o in range(4):
            xx = lax.rem(x + o, 4)
            piece = tot.at[phase, pl.ds(pl.multiple_of(xx * 16, 16), 16)]
            c = copy(
                piece, back.at[me], fin_s.at[phase, o], fin_r.at[me], device(xx, z, phase)
            )
            if o:
                start(c)
            else:
                @pl.when(core != phase)
                def _():
                    c.start()

                @pl.when(core == phase)
                def _():
                    back[me] = tot[phase, my_rows, :]

    def wgrad(first, count):
        @pl.loop(first, first + count)
        def _(t):
            q = lax.div(t, quarter // 256)
            cols = pl.ds(pl.multiple_of(lax.rem(t, quarter // 256) * 256, 256), 256)
            left = a_ref[q, :, :, :, cols].reshape(-1, 256)
            right = carried[...].reshape(-1, width)
            d = lax.dot_general(left, right, (((0,), (0,)), ((), ())), preferred_element_type=F32)
            rows = pl.ds(pl.multiple_of(t * 256, 256), 256)
            wg[rows, :] = d.astype(BF)

        rows = pl.ds(first * 256, count * 256)
        c = pltpu.make_async_copy(wg.at[rows], grad_hbm.at[rows], wg_sem.at[len(copies)])
        c.start()
        copies.append(c)

    def vec_copy(t):
        return copy(v_out.at[t], v_in.at[t], v_s.at[t], v_r.at[t], doubling[t])

    def vec_next(t):
        vec_copy(t).wait_recv()
        v_out[t + 1] = v_out[t] + v_in[t]
        start(vec_copy(t + 1))

    half_model = model // 2
    copies = []

    for phase in (0, 1):
        group_wait(phase)
        ag_send(phase, UP, 0)
        ag_send(phase, DOWN, 0)
        sib_send(phase, 0)
    w_copy.wait()
    mm1(0)
    for j in range(1, 5):
        forward(0, j)
        forward(1, j)
        if j == 1:
            mm1(1, 2)
            mid1(0)
        elif j == 2:
            mm1(3, 4)
            mid2(0)
            mid1(1)
            mid1(2)
        elif j == 3:
            mm1(5, 6)
            mid2(1)
            mid2(2)
            mid1(3)
            mid1(4)
            mm2(0)
        else:
            mm1(7)
            mid1(5)
            mid1(6)
            mid2(3)
            mid2(4)
            mm2(1, 2)
    mid1(7)
    mid2(5)
    mid2(6)
    mm2(3, 4)
    mid2(7)
    mm2(5, 6)
    x_step(0, 5)
    x_step(1, 3)
    mm2(7)

    @pl.when(leading)
    def _():
        gains = vec_ref[:, pl.ds(pl.multiple_of(rep * half_model, 128), half_model)]
        v_out[0] = v_out[0] / gains

    @pl.when(jnp.logical_not(leading))
    def _():
        for q in range(2):
            line = jnp.zeros((1, quarter), F32)
            for xx in (xlo, xlo + 2):
                rows = pl.ds(pl.multiple_of(xx * 16, 16), 16)
                line += jnp.sum(a_ref[q, core, z, rows].astype(F32), axis=0, keepdims=True)
            v_out[0, :, q * quarter:(q + 1) * quarter] = line

    start(vec_copy(0))
    x_step(0, 4)
    x_step(1, 4)
    rs_step(0, DOWN, 0)
    rs_step(1, UP, 0)
    vec_next(0)
    x_step(0, 6)
    x_step(1, 2)
    rs_step(0, UP, 0)
    rs_step(1, DOWN, 0)
    x_step(0, 3)
    x_step(1, 5)
    rs_step(0, DOWN, 1)
    rs_step(1, UP, 1)
    vec_next(1)
    x_step(0, 7)
    x_step(1, 1)
    wgrad(0, 2)
    rs_step(0, UP, 1)
    rs_step(1, DOWN, 1)
    x_step(0, 2)
    x_step(1, 6)
    rs_step(0, DOWN, 2)
    rs_step(1, UP, 2)
    vec_next(2)
    x_step(0, 1)
    x_step(1, 7)
    wgrad(2, 2)
    rs_step(0, UP, 2)
    rs_step(1, DOWN, 2)
    vec_next(3)
    x_step(0, 0)
    x_step(1, 0)
    wgrad(4, 2)
    rs_step(0, UP, 3)
    rs_step(1, DOWN, 3)
    vec_next(4)
    wgrad(6, 3)
    rs_final(0)
    rs_final(1)
    wgrad(9, 3)

    copy(rows_ref, resid, resid_sem.at[0], resid_sem.at[1], sec_mate).wait_recv()
    for o in range(1, 8):
        j = lax.rem(me + o, 8)
        copy(back.at[j], back.at[j], fin_s.at[0, 0], fin_r.at[j], member(j)).wait_recv()

    def quarter_sum(q):
        j = (q // 2) * 4 + q % 2
        return jnp.concatenate([
            back[j, :, both].astype(F32) + back[j + 2, :, both].astype(F32),
            back[j, :, mine_to].astype(F32),
            back[j + 2, :, mine_to].astype(F32),
        ], axis=1)

    @pl.when(leading)
    def _():
        mean = jnp.zeros((16, 1), F32)
        mix = jnp.zeros((16, 1), F32)
        for q in range(4):
            cols = slice(q * quarter, (q + 1) * quarter)
            s = quarter_sum(q)
            std = standard[:, cols]
            g = s * vec_ref[:, cols]
            summed[:, cols] = g
            mean += jnp.sum(g, axis=1, keepdims=True)
            mix += jnp.sum(g * std, axis=1, keepdims=True)
        mean = mean / model
        mix = mix / model
        rs = scale[:, 0:1]
        for q in range(4):
            cols = slice(q * quarter, (q + 1) * quarter)
            through = (summed[:, cols] - mean - standard[:, cols] * mix) * rs
            leave_ref[:, cols] = (resid[:, cols].astype(F32) + through).astype(BF)

    @pl.when(jnp.logical_not(leading))
    def _():
        for q in range(4):
            cols = slice(q * quarter, (q + 1) * quarter)
            leave_ref[:, cols] = (resid[:, cols].astype(F32) + quarter_sum(q) + vec_ref[:, cols]).astype(BF)

    vec_copy(5).wait_recv()
    mine = pl.ds(pl.multiple_of(rep * half_model, 128), half_model)
    other = pl.ds(pl.multiple_of((1 - rep) * half_model, 128), half_model)
    total_ref[:, mine] = v_out[5]
    total_ref[:, other] = v_in[5]

    for c in sent:
        c.wait_send()
    for phase in (0, 1):
        @pl.when(core != phase)
        def _():
            copy(
                tot.at[phase, my_rows], back.at[me], fin_s.at[phase, 0], fin_r.at[me], device(x, z, phase)
            ).wait_send()
    for c in copies:
        c.wait()


def local(weights, arriving, vectors):
    _, half, width = weights.shape
    _, micro, rows, model = arriving.shape
    quarter = model // 4
    dma = pltpu.SemaphoreType.DMA
    vm = pltpu.VMEM
    block = (64, quarter)
    third = quarter // 3
    leaving, weight_grad, totals = pl.pallas_call(
        kernel,
        out_shape=(
            jax.ShapeDtypeStruct((micro * rows, model), BF),
            jax.ShapeDtypeStruct((half, width), BF),
            jax.ShapeDtypeStruct((1, model), F32),
        ),
        in_specs=[
            pl.BlockSpec(memory_space=pl.ANY),
            pl.BlockSpec(memory_space=pltpu.VMEM),
            pl.BlockSpec(memory_space=pltpu.VMEM),
        ],
        out_specs=(
            pl.BlockSpec(memory_space=pltpu.VMEM),
            pl.BlockSpec(memory_space=pl.ANY),
            pl.BlockSpec(memory_space=pltpu.VMEM),
        ),
        scratch_shapes=[
            vm((half, width), BF),
            vm((4, 16, quarter), BF),
            vm((16, model), F32),
            vm((16, 128), F32),
            vm((16, model), BF),
            vm((2, 2, NZ, *block), BF),
            vm((8, 128, width), F32),
            vm((8, 128, width), BF),
            vm((8, 64, width), BF),
            vm((8, 64, width), BF),
            vm((8, 64, width), BF),
            vm((2, NZ, 64, width), BF),
            vm((2, NZ, *block), BF),
            vm((2, NZ, *block), BF),
            vm((2, NZ, *block), BF),
            vm((2, NZ, 64, third), BF),
            vm((2, NZ, 64, third), BF),
            vm((2, 2, 4, 64, 2 * third), BF),
            vm((half, width), BF),
            vm((2, 64, 2 * third), BF),
            vm((8, 16, 2 * third), BF),
            vm((16, model), F32),
            vm((6, 1, half), F32),
            vm((6, 1, half), F32),
            dma, dma((5,)), dma((8,)), dma((8,)), dma((2,)),
            dma((2, 2, 4)), dma((2, 2, 4)), dma((2, NZ)), dma((2, NZ)),
            dma((8,)), dma((8,)), dma((8,)), dma((8,)), dma((8,)), dma((8,)),
            dma((2, NZ)), dma((2, NZ)), dma((2, NZ)), dma((2, NZ)), dma((2, 2, 4)), dma((2, 2, 4)),
            dma((2, 4)), dma((8,)),
            dma((6,)), dma((6,)),
        ],
        compiler_params=pltpu.CompilerParams(
            collective_id=0, has_side_effects=True, vmem_limit_bytes=46 * 1024 * 1024
        ),
        cost_estimate=pl.CostEstimate(
            flops=3 * 2 * 1024 * half * width, bytes_accessed=4 * half * width, transcendentals=1024 * width
        ),
    )(weights[0], arriving[0].reshape(micro * rows, model), vectors)
    return (leaving.reshape(1, micro, rows, model), weight_grad[None], totals)


def solution(mesh):
    placed = (
        P("section", "dp", "tensor"),
        P("section", None, ("dp", "tensor"), None),
        P("section", None),
    )
    return jax.shard_map(
        local,
        mesh=mesh,
        in_specs=placed,
        out_specs=(
            P("section", None, ("dp", "tensor"), None),
            P("section", "dp", "tensor"),
            P("section", None),
        ),
        check_vma=False,
    )
```
